256 devices in a mesh: row: 32 (over x_hi, z, core), rep: 8 (over x_lo, y).
Axes of the slice: x: 4 (x_hi: 2, x_lo: 2; x = x_hi * 2 + x_lo), y: 4, z: 8, core: 2. Of those that a mesh axis runs over, the one named last changes fastest.
Arguments:
- features: bfloat16 [32768, 128], P('row'), may hold values from -6 to 6
- adj_tiles: bfloat16 [32, 8, 4, 32, 128, 128], P('row', 'rep'), may hold values from -0.0625 to 0.0625
- tile_coords: int32 [32, 8, 4, 32, 2], P('row', 'rep'), may hold values from 0 to 7, as said below
- tile_counts: int32 [32, 8, 4], P('row', 'rep'), may hold values from 1 to 32, as said below
- weight: bfloat16 [128, 256], replicated, may hold values from -0.5 to 0.5
- out_bias: float32 [256], replicated, may hold values from -3 to 3
- out_grad: bfloat16 [32768, 256], P(('row', 'rep')), may hold values from -0.032958984 to 0.032958984
Outputs:
- activated: bfloat16 [32768, 256], P(('row', 'rep'))
- weight_grad: float32 [128, 256], replicated
- bias_grad: float32 [256], replicated
The draws below stay inside these ranges and needn't reach their ends.
Inputs may be any that keep to these rules, and one draw needn't show every extreme that they name: `tile_coords`: within one block pair the live slots name distinct tiles; dead slots name valid tiles too. `tile_counts`: some block pair is full in every draw.
All inputs are finite; a program needn't handle non-finite values.
Results may differ from the reference program's by a relative error of at most 0.007.
Values may be sent and summed in bfloat16 or wider, within the bound.
A program may use at most 64 MiB of HBM per device.

```python
import jax
import jax.numpy as jnp
from jax import lax

TILE = 128
F_IN = 128
HID = 256
BLK_DEV = 8
CAP = 32
SECTIONS = 4
NODES = 32768
N_ROW = 32
N_REP = 8


def draw_tile_coords(key, part):
    key = jax.random.fold_in(key, 11)
    pairs = BLK_DEV * BLK_DEV
    scores = jax.random.randint(key, (N_ROW, N_REP, SECTIONS, pairs), 0, 4096) * pairs + jnp.arange(pairs).astype(jnp.int32)
    order = jnp.argsort(scores, axis=-1, stable=True)[..., :CAP].astype(jnp.int32)
    return jnp.stack([order // BLK_DEV, order % BLK_DEV], axis=-1).astype(jnp.int32)


def draw_tile_counts(key, part):
    key = jax.random.fold_in(key, 23)
    key_level, key_count, key_full = jax.random.split(key, 3)
    level = jax.random.randint(key_level, (N_ROW, N_REP, 1), 0, 4)
    raw_count = jax.random.randint(key_count, (N_ROW, N_REP, SECTIONS), max(1, CAP // 4), CAP + 1)
    counts = jnp.maximum(1, raw_count * (4 + level) // 7)
    full_at = jax.random.randint(key_full, (), 0, N_ROW * N_REP * SECTIONS)
    flat_index = jnp.arange(N_ROW * N_REP * SECTIONS).reshape(N_ROW, N_REP, SECTIONS)
    return jnp.where(flat_index == full_at, CAP, counts).astype(jnp.int32)


def block_scale(rng, shape, pieces, smallest, largest):
    loudness = 1.0
    for position, shards_of in pieces:
        steps = jax.random.uniform(jax.random.fold_in(jax.random.fold_in(rng, 6), position), (shards_of,), jnp.float32, smallest / len(pieces), largest / len(pieces))
        loudness = loudness * jnp.repeat(jnp.exp(steps), shape[position] // shards_of).reshape((-1,) + (1,) * (len(shape) - 1 - position))
    return loudness


def bell_draw(stream_key, extent, deviation, most, pieces=(), kind=jnp.bfloat16):
    loudness = block_scale(stream_key, extent, pieces, -0.22, 0.18) if pieces else 1.0
    values = jax.random.normal(stream_key, extent, jnp.float32) * deviation * loudness
    return jnp.minimum(jnp.maximum(values, -most), most).astype(kind)


def setup_inputs(seed: int = 0) -> dict:
    streams_of = jax.random.split(jax.random.key(seed), 8)
    features = bell_draw(streams_of[0], (NODES, F_IN), 1.0, 6.0, ((0, 32),))
    adj_tiles = bell_draw(streams_of[1], (N_ROW, N_REP, SECTIONS, CAP, TILE, TILE), (N_ROW * CAP * TILE // (2 * BLK_DEV)) ** -0.5, 0.0625, ((0, 32), (1, 8)))
    tile_coords = draw_tile_coords(jax.random.fold_in(streams_of[7], 71), 0)
    tile_counts = draw_tile_counts(jax.random.fold_in(streams_of[7], 71), 0)
    weight = bell_draw(streams_of[4], (F_IN, HID), F_IN ** -0.5, 0.5)
    out_bias = bell_draw(streams_of[5], (HID,), 0.5, 3.0, (), jnp.float32)
    out_grad = bell_draw(streams_of[6], (NODES, HID), (NODES ** -0.5), 0.032958984, ((0, 256),))
    return dict(features=features, adj_tiles=adj_tiles, tile_coords=tile_coords, tile_counts=tile_counts, weight=weight, out_bias=out_bias, out_grad=out_grad)


def reference(features, adj_tiles, tile_coords, tile_counts, weight, out_bias, out_grad):
    x_blocks = features.reshape(N_ROW, BLK_DEV, TILE, F_IN)
    section_block = (jnp.arange(SECTIONS)[None, :] * N_REP + jnp.arange(N_REP)[:, None]).astype(jnp.int32)
    position_index = jnp.arange(CAP).astype(jnp.int32)
    row_index = jnp.arange(BLK_DEV).astype(jnp.int32)

    def one_block(operands):
        blk_tiles, coords, counts = operands
        live_mask = position_index[None, None, :] < counts[:, :, None]
        selected_entries = x_blocks[section_block[:, :, None], coords[..., 1]]
        tile_products = jnp.einsum("jtcab,jtcbf->jtcaf", blk_tiles.astype(jnp.float32), selected_entries.astype(jnp.float32), precision=lax.Precision.HIGHEST)
        placement = ((coords[..., 0][..., None] == row_index) & live_mask[..., None]).astype(jnp.float32)
        reduced_total = jnp.einsum("jtcr,jtcaf->raf", placement, tile_products, precision=lax.Precision.HIGHEST)
        return reduced_total.reshape(BLK_DEV * TILE, F_IN)

    partial_rows = lax.map(one_block, (adj_tiles, tile_coords, tile_counts))
    aggregated = partial_rows.reshape(NODES, F_IN).astype(jnp.bfloat16)
    pre_act = jnp.dot(aggregated, weight, preferred_element_type=jnp.float32) + out_bias
    activated = jax.nn.silu(pre_act).astype(jnp.bfloat16)
    sigmoid_pre = jax.nn.sigmoid(pre_act)
    grad_pre = (out_grad.astype(jnp.float32) * sigmoid_pre * (1.0 + pre_act * (1.0 - sigmoid_pre))).astype(jnp.bfloat16)
    weight_grad = jnp.dot(aggregated.T, grad_pre, preferred_element_type=jnp.float32)
    bias_grad = jnp.sum(grad_pre.astype(jnp.float32), axis=0)
    return activated, weight_grad, bias_grad
```

```python
import functools

import jax
import jax.numpy as jnp
from jax import lax
from jax.experimental import pallas as pl
from jax.experimental.pallas import tpu as pltpu
from jax.sharding import PartitionSpec as P

MESH = pl.DeviceIdType.MESH
F32 = jnp.float32
BF16 = jnp.bfloat16

PLANE = sorted(
    [(dx, dy) for dx in range(4) for dy in range(4) if (dx, dy) != (0, 0)],
    key=lambda o: -(min(o[0], 4 - o[0]) + min(o[1], 4 - o[1])),
)
ALONG_Z = [4, 3, 5, 2, 6, 1, 7]
COLUMN = [(d, k) for d in ALONG_Z for k in (0, 1)] + [(0, 1)]


def layer_kernel(
    inv_ref,
    feat_ref,
    adj_ref,
    weight_ref,
    bias_ref,
    cot_ref,
    act_ref,
    wg_ref,
    bg_ref,
    tiles,
    held,
    feats,
    acc,
    part_out,
    part_in,
    c1_out,
    c1_in,
    c2_in,
    c3_in,
    tile_sem,
    a1_send,
    a1_recv,
    a2_send,
    a2_recv,
    a3_send,
    b_send,
    b_recv,
    c_send,
    c_recv,
):
    row = lax.axis_index("row")
    rep = lax.axis_index("rep")
    xh, z, core = row // 16, (row // 2) % 8, row % 2
    x, y = xh * 2 + rep // 4, rep % 4
    plane = x * 4 + y
    column = z * 2 + core

    def device(dx, dy, dz, dcore):
        x2, y2, z2, c2 = (x + dx) % 4, (y + dy) % 4, (z + dz) % 8, (core + dcore) % 2
        return (x2 // 2) * 16 + z2 * 2 + c2, (x2 % 2) * 4 + y2

    def remote(src, dst, send, recv, target):
        return pltpu.make_async_remote_copy(
            src_ref=src,
            dst_ref=dst,
            send_sem=send,
            recv_sem=recv,
            device_id=target,
            device_id_type=MESH,
        )

    def wait_bytes(ref, sem):
        pltpu.make_async_copy(ref, ref, sem).wait()

    live = tiles.shape[0] - 1
    tile_copy = pltpu.make_async_copy(adj_ref, tiles.at[pl.ds(0, live)], tile_sem)
    tile_copy.start()

    barrier = pltpu.get_barrier_semaphore()
    for dx, dy in PLANE:
        pl.semaphore_signal(barrier, inc=1, device_id=device(dx, dy, 0, 0), device_id_type=MESH)
    for dz, dcore in COLUMN:
        pl.semaphore_signal(barrier, inc=1, device_id=device(0, 0, dz, dcore), device_id_type=MESH)
    tiles[live] = jnp.zeros(tiles.shape[1:], BF16)
    c1_out[...] = jnp.zeros_like(c1_out)
    held[z % 4, z // 4] = feat_ref[rep]
    pl.semaphore_wait(barrier, len(PLANE) + len(COLUMN))

    sends = []
    for dz in ALONG_Z:
        copy = remote(
            feat_ref.at[rep], held.at[z % 4, z // 4], a1_send, a1_recv.at[z], device(0, 0, dz, 0)
        )
        copy.start()
        sends.append(copy)

    def to_users(step, target_xh):
        m = (z + step) % 4
        user = m * 2 + core
        mine = jnp.logical_and(user == rep, xh == target_xh)
        copy = remote(
            held.at[m],
            feats.at[pl.ds(xh * 2, 2), rep],
            a2_send,
            a2_recv.at[xh, rep],
            (target_xh * 16 + z * 2 + core, user),
        )
        local = pltpu.make_async_copy(
            held.at[m], feats.at[pl.ds(xh * 2, 2), rep], a2_recv.at[xh, rep]
        )
        return mine, copy, local

    for step in (0, 2, 1, 3):
        for half in (0, 4):
            dz = (step + half) % 8
            if dz:
                src = (z + dz) % 8
                wait_bytes(held.at[src % 4, src // 4], a1_recv.at[src])
        for target_xh in (0, 1):
            mine, copy, local = to_users(step, target_xh)

            @pl.when(jnp.logical_not(mine))
            def _():
                copy.start()

            @pl.when(mine)
            def _():
                local.start()

    primary = core == y % 2

    def pass_on(src_xh, q):
        piece = feats.at[pl.ds(src_xh * 2, 2), q]
        return remote(piece, piece, a3_send, a2_recv.at[src_xh, q], device(0, 0, 0, 1))

    tile_copy.wait()
    for src_xh in (0, 1):
        for q in range(8):
            wait_bytes(feats.at[pl.ds(src_xh * 2, 2), q], a2_recv.at[src_xh, q])

            @pl.when(primary)
            def _():
                pass_on(src_xh, q).start()

    def products(r, sections):
        total = None
        for t in sections:
            left = jnp.concatenate([tiles[inv_ref[t * 64 + r * 8 + q]] for q in range(8)], axis=1)
            right = feats[t].reshape(8 * 128, 128)
            term = jnp.dot(left, right, preferred_element_type=F32)
            total = term if total is None else total + term
        return total

    def send_part(r):
        return remote(part_out.at[r], part_in.at[rep], b_send, b_recv, (row, r))

    def tile_row(i, carry):
        r = (rep + 1 + i) % 8
        total = products(r, range(4))
        acc[r] = total
        part_out[r] = total.astype(BF16)

        @pl.when(r != rep)
        def _():
            send_part(r).start()

        return carry

    lax.fori_loop(0, 8, tile_row, 0)
    part_in[rep] = jnp.zeros(part_in.shape[1:], BF16)
    wait_bytes(part_in.at[pl.ds(0, 7)], b_recv)
    total = acc[rep]
    for s in range(8):
        total = total + part_in[s].astype(F32)

    aggregated = total.astype(BF16)
    pre = jnp.dot(aggregated, weight_ref[...], preferred_element_type=F32) + bias_ref[...]
    sig = jax.nn.sigmoid(pre)
    act_ref[...] = (pre * sig).astype(BF16)
    grad = (cot_ref[...].astype(F32) * sig * (1.0 + pre * (1.0 - sig))).astype(BF16)
    weight_part = lax.dot_general(
        aggregated, grad, (((0,), (0,)), ((), ())), preferred_element_type=F32
    )
    bias_part = jnp.sum(grad.astype(F32), axis=0, keepdims=True)

    c1_out[:, :, 0:256] = weight_part.reshape(16, 8, 256)
    for p in range(16):
        c1_out[p, 0:1, 256:384] = bias_part[:, 0:128]
        c1_out[p, 1:2, 256:384] = bias_part[:, 128:256]
    for dx, dy in PLANE:
        p = ((x + dx) % 4) * 4 + (y + dy) % 4
        remote(
            c1_out.at[p], c1_in.at[plane], c_send.at[0], c_recv.at[0], device(dx, dy, 0, 0)
        ).start()
    c1_in[plane] = c1_out[plane]
    wait_bytes(c1_in.at[pl.ds(0, 15)], c_recv.at[0])
    c2_in[column] = jnp.sum(c1_in[...], axis=0)
    for dz, dcore in COLUMN:
        remote(
            c2_in.at[column], c2_in.at[column], c_send.at[1], c_recv.at[1], device(0, 0, dz, dcore)
        ).start()
    wait_bytes(c2_in.at[pl.ds(0, 15)], c_recv.at[1])
    summed = jnp.sum(c2_in[...], axis=0)
    c3_in[plane] = summed[:, 0:256]
    for dx, dy in PLANE:
        remote(
            c3_in.at[plane], c3_in.at[plane], c_send.at[2], c_recv.at[2], device(dx, dy, 0, 0)
        ).start()
    bg_ref[:, 0:128] = summed[0:1, 256:384]
    bg_ref[:, 128:256] = summed[1:2, 256:384]
    wait_bytes(c3_in.at[pl.ds(0, 15)], c_recv.at[2])
    wg_ref[...] = c3_in[...].reshape(128, 256)

    for copy in sends:
        copy.wait_send()
    for step in (0, 2, 1, 3):
        for target_xh in (0, 1):
            mine, copy, local = to_users(step, target_xh)

            @pl.when(jnp.logical_not(mine))
            def _():
                copy.wait_send()

    @pl.when(primary)
    def _():
        for src_xh in (0, 1):
            for q in range(8):
                pass_on(src_xh, q).wait_send()

    wait_bytes(part_out.at[pl.ds(0, 7)], b_send)
    wait_bytes(c1_out.at[pl.ds(0, 15)], c_send.at[0])
    wait_bytes(c2_in.at[pl.ds(0, 15)], c_send.at[1])
    wait_bytes(c3_in.at[pl.ds(0, 15)], c_send.at[2])


def slot_of_tile(coords, counts):
    sections, slots = coords.shape[0], coords.shape[1]
    key = coords[:, :, 0] * 8 + coords[:, :, 1]
    live = jnp.arange(slots)[None, :] < counts[:, None]
    slot = jnp.arange(sections)[:, None] * slots + jnp.arange(slots)[None, :] - sections * slots
    hit = (key[:, None, :] == jnp.arange(64)[None, :, None]) & live[:, None, :]
    found = jnp.sum(jnp.where(hit, slot[:, None, :], 0), axis=-1) + sections * slots
    return found.reshape(sections * 64).astype(jnp.int32)


def shards(features, adj_tiles, tile_coords, tile_counts, weight, out_bias, out_grad):
    inv = slot_of_tile(tile_coords[0, 0], tile_counts[0, 0])
    vmem = pl.BlockSpec(memory_space=pltpu.VMEM)
    dma = pltpu.SemaphoreType.DMA
    activated, weight_grad, bias_grad = pl.pallas_call(
        layer_kernel,
        name="layer",
        out_shape=(
            jax.ShapeDtypeStruct((128, 256), BF16),
            jax.ShapeDtypeStruct((128, 256), F32),
            jax.ShapeDtypeStruct((1, 256), F32),
        ),
        in_specs=[
            pl.BlockSpec(memory_space=pltpu.SMEM),
            vmem,
            pl.BlockSpec(memory_space=pl.ANY),
            vmem,
            vmem,
            vmem,
        ],
        out_specs=(vmem, vmem, vmem),
        scratch_shapes=[
            pltpu.VMEM((129, 128, 128), BF16),
            pltpu.VMEM((4, 2, 128, 128), BF16),
            pltpu.VMEM((4, 8, 128, 128), BF16),
            pltpu.VMEM((8, 128, 128), F32),
            pltpu.VMEM((8, 128, 128), BF16),
            pltpu.VMEM((8, 128, 128), BF16),
            pltpu.VMEM((16, 8, 384), F32),
            pltpu.VMEM((16, 8, 384), F32),
            pltpu.VMEM((16, 8, 384), F32),
            pltpu.VMEM((16, 8, 256), F32),
            dma,
            dma,
            dma((8,)),
            dma,
            dma((2, 8)),
            dma,
            dma,
            dma,
            dma((3,)),
            dma((3,)),
        ],
        compiler_params=pltpu.CompilerParams(
            collective_id=1, has_side_effects=True, vmem_limit_bytes=56 << 20
        ),
        cost_estimate=pl.CostEstimate(
            flops=2 * 256 * 128**3, bytes_accessed=5 << 20, transcendentals=128 * 256
        ),
    )(
        inv,
        features.reshape(8, 128, 128),
        adj_tiles.reshape(128, 128, 128),
        weight,
        out_bias.reshape(1, 256),
        out_grad,
    )
    return activated, weight_grad, bias_grad.reshape(256)


def solution(mesh):
    placed = (
        P("row", None),
        P("row", "rep", None, None, None, None),
        P("row", "rep", None, None, None),
        P("row", "rep", None),
        P(),
        P(),
        P(("row", "rep"), None),
    )
    return jax.shard_map(
        shards,
        mesh=mesh,
        in_specs=placed,
        out_specs=(P(("row", "rep"), None), P(), P()),
        check_vma=False,
    )
```

```python
import functools

import jax
import jax.numpy as jnp
from jax import lax
from jax.experimental import pallas as pl
from jax.experimental.pallas import tpu as pltpu
from jax.sharding import PartitionSpec as P

MESH = pl.DeviceIdType.MESH
F32 = jnp.float32
BF16 = jnp.bfloat16

PLANE = sorted(
    [(dx, dy) for dx in range(4) for dy in range(4) if (dx, dy) != (0, 0)],
    key=lambda o: -(min(o[0], 4 - o[0]) + min(o[1], 4 - o[1])),
)
COLUMN = [(d, k) for d in (4, 3, 5, 2, 6, 1, 7) for k in (0, 1)] + [(0, 1)]


def layer_kernel(
    counts_ref,
    coords_ref,
    feat_ref,
    adj_ref,
    weight_ref,
    bias_ref,
    cot_ref,
    act_ref,
    wg_ref,
    bg_ref,
    tiles,
    slot_rows,
    slots,
    held,
    feats,
    acc,
    part_out,
    part_in,
    c1_out,
    c1_in,
    b1_out,
    b1_in,
    c2_in,
    c3_in,
    tile_sem,
    slot_sem,
    a1_send,
    a1_recv,
    a2_send,
    a2_recv,
    a3_send,
    b_send,
    b_recv,
    c_send,
    c_recv,
):
    row = lax.axis_index("row")
    rep = lax.axis_index("rep")
    xh, z, core = row // 16, (row // 2) % 8, row % 2
    xl, y = rep // 4, rep % 4
    x = xh * 2 + xl
    plane = x * 4 + y
    column = z * 2 + core
    live = tiles.shape[0] - 1

    def device(dx, dy, dz, dcore):
        x2, y2, z2, c2 = (x + dx) % 4, (y + dy) % 4, (z + dz) % 8, (core + dcore) % 2
        return (x2 // 2) * 16 + z2 * 2 + c2, (x2 % 2) * 4 + y2

    def remote(src, dst, send, recv, target):
        return pltpu.make_async_remote_copy(
            src_ref=src,
            dst_ref=dst,
            send_sem=send,
            recv_sem=recv,
            device_id=target,
            device_id_type=MESH,
        )

    def wait_bytes(ref, sem):
        pltpu.make_async_copy(ref, ref, sem).wait()

    pending = []
    tile_copy = pltpu.make_async_copy(adj_ref, tiles.at[pl.ds(0, live)], tile_sem)
    tile_copy.start()

    barrier = pltpu.get_barrier_semaphore()
    for dz, dcore in COLUMN:
        pl.semaphore_signal(barrier, inc=1, device_id=device(0, 0, dz, dcore), device_id_type=MESH)
    for dx, dy in PLANE:
        pl.semaphore_signal(barrier, inc=1, device_id=device(dx, dy, 0, 0), device_id_type=MESH)

    tiles[live] = jnp.zeros(tiles.shape[1:], BF16)
    lane = lax.broadcasted_iota(jnp.int32, (64, 32), 1)
    sub = lax.broadcasted_iota(jnp.int32, (64, 32), 0)
    wide_lane = lax.broadcasted_iota(jnp.int32, (64, 128), 1)
    wide_sub = lax.broadcasted_iota(jnp.int32, (64, 128), 0)
    for t in range(4):
        key = coords_ref[t, 0:1, :] * 8 + coords_ref[t, 1:2, :]
        hit = jnp.logical_and(key == sub, lane < counts_ref[t])
        found = jnp.sum(jnp.where(hit, lane + (t * 32 + 1), 0), axis=1, keepdims=True)
        turned = jnp.sum(jnp.where(wide_lane == wide_sub, found, 0), axis=0, keepdims=True)
        slot_rows[t : t + 1, :] = jnp.where(turned == 0, live, turned - 1)
    slot_copy = pltpu.make_async_copy(slot_rows, slots, slot_sem)
    slot_copy.start()

    flip = (core + xh) % 2

    @pl.when(xh == 0)
    def _():
        held[z] = feat_ref[rep]

    b1_out[...] = jnp.zeros_like(b1_out)
    part_in[rep] = jnp.zeros(part_in.shape[1:], BF16)
    pl.semaphore_wait(barrier, len(PLANE) + len(COLUMN))

    def along_z(dz):
        place = held.at[z]
        return remote(feat_ref.at[rep], place, a1_send.at[dz], a1_recv.at[z], device(0, 0, dz, xh))

    def pass_along(dz, to, first, rows):
        src = (z + dz) % 8
        piece = held.at[src, pl.ds(first, rows)]
        return remote(piece, piece, a1_send.at[8 + to % 8], a1_recv.at[src], device(0, 0, to, 0))

    def launch(copy):
        copy.start()
        pending.append(copy.wait_send)

    @pl.when(xh == 1)
    def _():
        along_z(0).start()

    pending.append(lambda: pl.when(xh == 1)(lambda: along_z(0).wait_send()))
    for dz in (2, 6, 1, 7):
        launch(along_z(dz))

    def to_user(dz, target_xh, start):
        src = (z + dz) % 8
        user = (src % 4) * 2 + flip
        mine = jnp.logical_and(user == rep, xh == target_xh)
        piece = held.at[src]
        section = xh * 2 + src // 4
        place = feats.at[section, rep]

        @pl.when(jnp.logical_not(mine))
        def _():
            copy = remote(
                piece,
                place,
                a2_send.at[dz, target_xh],
                a2_recv.at[section],
                (target_xh * 16 + z * 2 + core, user),
            )
            if start:
                copy.start()
            else:
                copy.wait_send()

        if start:

            @pl.when(mine)
            def _():
                pltpu.make_async_copy(piece, place, a2_recv.at[section]).start()

    def to_users(dz):
        for target_xh in (0, 1):
            to_user(dz, target_xh, True)
            pending.append(functools.partial(to_user, dz, target_xh, False))

    def wait_piece(dz):
        src = (z + dz) % 8
        wait_bytes(held.at[src], a1_recv.at[src])

    pl.when(xh == 1)(lambda: wait_piece(0))
    to_users(0)
    wait_piece(2)
    launch(pass_along(2, -2, 0, 64))
    launch(pass_along(2, -1, 0, 128))
    wait_piece(6)
    launch(pass_along(6, 2, 64, 64))
    launch(pass_along(6, 1, 0, 128))
    for dz in (1, 7):
        wait_piece(dz)
        to_users(dz)
    for dz in (2, 6):
        to_users(dz)
    for dz in (3, 5, 4):
        wait_piece(dz)
        to_users(dz)

    mine_xh = (core + y) % 2
    nearer = ((rep // 2 - z + 10) % 8) // 5
    own = [mine_xh * 2 + nearer, mine_xh * 2 + 1 - nearer]
    other = [2 - mine_xh * 2 + nearer, 3 - mine_xh * 2 - nearer]

    def arrive(section):
        wait_bytes(feats.at[section], a2_recv.at[section])

    def pass_on(section):
        piece = feats.at[section]
        launch(remote(piece, piece, a3_send.at[section], a2_recv.at[section], device(0, 0, 0, 1)))

    def products(r, section):
        left = jnp.concatenate([tiles[slots[section, r * 8 + q]] for q in range(8)], axis=1)
        right = feats[section].reshape(8 * 128, 128)
        return jnp.dot(left, right, preferred_element_type=F32)

    def add_products(section, first):
        for r in range(8):
            term = products(r, section)
            acc[r] = term if first else acc[r] + term

    tile_copy.wait()
    slot_copy.wait()
    arrive(own[0])
    pass_on(own[0])
    add_products(own[0], True)
    arrive(own[1])
    pass_on(own[1])
    arrive(other[0])
    add_products(other[0], False)
    add_products(own[1], False)
    arrive(other[1])

    for i, k in enumerate((2, 1, 3, 0, 2, 1, 3, 0)):
        r = ((xl + 1 - i // 4) % 2) * 4 + (y + k) % 4
        total = acc[r] + products(r, other[1])
        if i < 7:
            part_out[r] = total.astype(BF16)
            remote(part_out.at[r], part_in.at[rep], b_send, b_recv, (row, r)).start()

    for finish in pending:
        finish()
    pending.clear()
    pending.append(lambda: wait_bytes(part_out.at[pl.ds(0, 7)], b_send))
    wait_bytes(part_in.at[pl.ds(0, 7)], b_recv)
    for s in range(8):
        total = total + part_in[s].astype(F32)

    aggregated = total.astype(BF16)
    pre = jnp.dot(aggregated, weight_ref[...], preferred_element_type=F32) + bias_ref[...]
    sig = jax.nn.sigmoid(pre)
    grad = (cot_ref[...].astype(F32) * sig * (1.0 + pre * (1.0 - sig))).astype(BF16)
    weight_part = lax.dot_general(
        aggregated, grad, (((0,), (0,)), ((), ())), preferred_element_type=F32
    )
    bias_part = jnp.sum(grad.astype(F32), axis=0, keepdims=True)

    owner = plane == 0
    c1_out[0:8] = weight_part[:, 0:128].astype(BF16).reshape(8, 16, 128)
    c1_out[8:16] = weight_part[:, 128:256].astype(BF16).reshape(8, 16, 128)
    b1_out[0:1, :] = bias_part[:, 0:128]
    b1_out[1:2, :] = bias_part[:, 128:256]

    def send_bias():
        return remote(
            b1_out, b1_in.at[plane], c_send.at[3], c_recv.at[3], (z * 2 + core, 0)
        )

    @pl.when(jnp.logical_not(owner))
    def _():
        send_bias().start()

    for dx, dy in PLANE:
        p = ((x + dx) % 4) * 4 + (y + dy) % 4
        remote(
            c1_out.at[p], c1_in.at[plane], c_send.at[0], c_recv.at[0], device(dx, dy, 0, 0)
        ).start()
    c1_in[plane] = c1_out[plane]
    act_ref[...] = (pre * sig).astype(BF16)
    for finish in pending:
        finish()
    pending.clear()
    pending.append(lambda: wait_bytes(c1_out.at[pl.ds(0, 15)], c_send.at[0]))
    pending.append(lambda: pl.when(jnp.logical_not(owner))(lambda: send_bias().wait_send()))
    wait_bytes(c1_in.at[pl.ds(0, 15)], c_recv.at[0])
    c2_in[column, 0:16] = jnp.sum(c1_in[...].astype(F32), axis=0).astype(BF16)

    def share_column(rows, start):
        piece = c2_in.at[column, pl.ds(0, rows)]
        for dz, dcore in COLUMN:
            remote(piece, piece, c_send.at[1], c_recv.at[1], device(0, 0, dz, dcore)).start()
        for finish in pending:
            finish()

    @pl.when(owner)
    def _():
        b1_in[0] = b1_out[...]
        wait_bytes(b1_in.at[pl.ds(0, 15)], c_recv.at[3])
        summed = jnp.sum(b1_in[...], axis=0)
        c2_in[column, 16:32] = jnp.concatenate([summed, jnp.zeros_like(summed)], axis=0).astype(BF16)
        share_column(32, True)
        wait_bytes(c2_in.at[pl.ds(0, 15)], c_recv.at[1])
        c3_in[0, 16:24] = jnp.sum(c2_in[:, 16:32].astype(F32), axis=0)[0:8]

    @pl.when(jnp.logical_not(owner))
    def _():
        share_column(16, True)
        wait_bytes(c2_in.at[pl.ds(0, 15), pl.ds(0, 16)], c_recv.at[1])

    pending.clear()

    @pending.append
    def _():
        pl.when(owner)(lambda: wait_bytes(c2_in.at[pl.ds(0, 15)], c_send.at[1]))
        pl.when(jnp.logical_not(owner))(
            lambda: wait_bytes(c2_in.at[pl.ds(0, 15), pl.ds(0, 16)], c_send.at[1])
        )

    c3_in[plane, 0:16] = jnp.sum(c2_in[:, 0:16].astype(F32), axis=0)

    @pl.when(owner)
    def _():
        for dx, dy in PLANE:
            remote(
                c3_in.at[0], c3_in.at[0], c_send.at[2], c_recv.at[4], device(dx, dy, 0, 0)
            ).start()
        for finish in pending:
            finish()
        wait_bytes(c3_in.at[pl.ds(0, 15), pl.ds(0, 16)], c_recv.at[2])

    @pl.when(jnp.logical_not(owner))
    def _():
        piece = c3_in.at[plane, pl.ds(0, 16)]
        for dx, dy in PLANE:
            remote(piece, piece, c_send.at[2], c_recv.at[2], device(dx, dy, 0, 0)).start()
        for finish in pending:
            finish()
        wait_bytes(c3_in.at[pl.ds(0, 14), pl.ds(0, 16)], c_recv.at[2])
        wait_bytes(c3_in.at[0], c_recv.at[4])

    pending.clear()

    @pending.append
    def _():
        pl.when(owner)(lambda: wait_bytes(c3_in.at[pl.ds(0, 15)], c_send.at[2]))
        pl.when(jnp.logical_not(owner))(
            lambda: wait_bytes(c3_in.at[pl.ds(0, 15), pl.ds(0, 16)], c_send.at[2])
        )

    wg_ref[:, 0:128] = c3_in[0:8, 0:16].reshape(128, 128)
    wg_ref[:, 128:256] = c3_in[8:16, 0:16].reshape(128, 128)
    bg_ref[:, 0:128] = c3_in[0, 16:17]
    bg_ref[:, 128:256] = c3_in[0, 17:18]

    for finish in pending:
        finish()


def hand_out(act_in, wg_in, bg_in, act_ref, wg_ref, bg_ref):
    act_ref[...] = act_in[...]
    wg_ref[...] = wg_in[...]
    bg_ref[...] = bg_in[...]


def shards(features, adj_tiles, tile_coords, tile_counts, weight, out_bias, out_grad):
    vmem = pl.BlockSpec(memory_space=pltpu.VMEM)
    dma = pltpu.SemaphoreType.DMA
    outs = (
        jax.ShapeDtypeStruct((128, 256), BF16),
        jax.ShapeDtypeStruct((128, 256), F32),
        jax.ShapeDtypeStruct((1, 256), F32),
    )
    results = pl.pallas_call(
        layer_kernel,
        name="layer",
        out_shape=outs,
        in_specs=[
            pl.BlockSpec(memory_space=pltpu.SMEM),
            vmem,
            vmem,
            pl.BlockSpec(memory_space=pl.ANY),
            vmem,
            vmem,
            vmem,
        ],
        out_specs=(vmem, vmem, vmem),
        scratch_shapes=[
            pltpu.VMEM((129, 128, 128), BF16),
            pltpu.VMEM((4, 128), jnp.int32),
            pltpu.SMEM((4, 128), jnp.int32),
            pltpu.VMEM((8, 128, 128), BF16),
            pltpu.VMEM((4, 8, 128, 128), BF16),
            pltpu.VMEM((8, 128, 128), F32),
            pltpu.VMEM((8, 128, 128), BF16),
            pltpu.VMEM((8, 128, 128), BF16),
            pltpu.VMEM((16, 16, 128), BF16),
            pltpu.VMEM((16, 16, 128), BF16),
            pltpu.VMEM((8, 128), F32),
            pltpu.VMEM((16, 8, 128), F32),
            pltpu.VMEM((16, 32, 128), BF16),
            pltpu.VMEM((16, 24, 128), F32),
            dma,
            dma,
            dma((16,)),
            dma((8,)),
            dma((8, 2)),
            dma((4,)),
            dma((4,)),
            dma,
            dma,
            dma((4,)),
            dma((5,)),
        ],
        compiler_params=pltpu.CompilerParams(
            collective_id=1, has_side_effects=True, vmem_limit_bytes=60 << 20
        ),
        cost_estimate=pl.CostEstimate(
            flops=2 * 256 * 128**3, bytes_accessed=5 << 20, transcendentals=128 * 256
        ),
    )(
        tile_counts.reshape(4),
        jnp.swapaxes(tile_coords[0, 0], 1, 2),
        features.reshape(8, 128, 128),
        adj_tiles.reshape(128, 128, 128),
        weight,
        out_bias.reshape(1, 256),
        out_grad,
    )
    activated, weight_grad, bias_grad = pl.pallas_call(
        hand_out,
        name="hand_out",
        out_shape=outs,
        in_specs=[vmem, vmem, vmem],
        out_specs=(vmem, vmem, vmem),
    )(*results)
    return activated, weight_grad, bias_grad.reshape(256)


def solution(mesh):
    placed = (
        P("row", None),
        P("row", "rep", None, None, None, None),
        P("row", "rep", None, None, None),
        P("row", "rep", None),
        P(),
        P(),
        P(("row", "rep"), None),
    )
    return jax.shard_map(
        shards,
        mesh=mesh,
        in_specs=placed,
        out_specs=(P(("row", "rep"), None), P(), P()),
        check_vma=False,
    )
```

```python
import functools

import jax
import jax.numpy as jnp
from jax import lax
from jax.experimental import pallas as pl
from jax.experimental.pallas import tpu as pltpu
from jax.sharding import PartitionSpec as P

MESH = pl.DeviceIdType.MESH
F32 = jnp.float32
BF16 = jnp.bfloat16

PLANE = sorted(
    [(dx, dy) for dx in range(4) for dy in range(4) if (dx, dy) != (0, 0)],
    key=lambda o: -(min(o[0], 4 - o[0]) + min(o[1], 4 - o[1])),
)
ALONG_Z = [4, 3, 5, 2, 6, 1, 7]
GREETED = [(0, 0, dz, dcore) for dz in (2, 6, 1, 7) for dcore in (0, 1)] + [(0, 0, 0, 1)]
GREETED += [(d, 0, 0, 0) for d in (2, 1, 3)] + [(0, d, 0, 0) for d in (2, 1, 3)]


def layer_kernel(
    counts_hbm,
    coords_hbm,
    feat_hbm,
    adj_hbm,
    weight_hbm,
    bias_hbm,
    cot_hbm,
    act_ref,
    wg_ref,
    bg_ref,
    counts_ref,
    coords_ref,
    weight_ref,
    bias_ref,
    cot_ref,
    tiles,
    slot_rows,
    slots,
    held,
    feats,
    acc,
    part_out,
    part_in,
    c1_out,
    c1_in,
    b1_out,
    b1_in,
    core_io,
    c2_in,
    c3_in,
    load_sem,
    slot_sem,
    a1_send,
    a1_recv,
    a2_send,
    a2_recv,
    a3_send,
    a3_recv,
    b_send,
    b_recv,
    c_send,
    c_recv,
):
    row = lax.axis_index("row")
    rep = lax.axis_index("rep")
    xh, z, core = row // 16, (row // 2) % 8, row % 2
    xl, y = rep // 4, rep % 4
    x = xh * 2 + xl
    plane = x * 4 + y
    live = tiles.shape[0] - 1

    def device(dx, dy, dz, dcore):
        x2, y2, z2, c2 = (x + dx) % 4, (y + dy) % 4, (z + dz) % 8, (core + dcore) % 2
        return (x2 // 2) * 16 + z2 * 2 + c2, (x2 % 2) * 4 + y2

    def remote(src, dst, send, recv, target):
        return pltpu.make_async_remote_copy(
            src_ref=src,
            dst_ref=dst,
            send_sem=send,
            recv_sem=recv,
            device_id=target,
            device_id_type=MESH,
        )

    def wait_bytes(ref, sem):
        pltpu.make_async_copy(ref, ref, sem).wait()

    barrier = pltpu.get_barrier_semaphore()
    for offset in GREETED:
        pl.semaphore_signal(barrier, inc=1, device_id=device(*offset), device_id_type=MESH)

    pending = []
    loads = [
        pltpu.make_async_copy(src, dst, load_sem.at[n])
        for n, (src, dst) in enumerate(
            [
                (counts_hbm, counts_ref),
                (coords_hbm, coords_ref),
                (adj_hbm, tiles.at[pl.ds(0, live)]),
                (weight_hbm, weight_ref),
                (bias_hbm, bias_ref),
                (cot_hbm, cot_ref),
            ]
        )
    ]
    for load in loads:
        load.start()
    tile_copy = loads[2]

    tiles[live] = jnp.zeros(tiles.shape[1:], BF16)
    lane = lax.broadcasted_iota(jnp.int32, (64, 32), 1)
    sub = lax.broadcasted_iota(jnp.int32, (64, 32), 0)
    wide_lane = lax.broadcasted_iota(jnp.int32, (64, 128), 1)
    wide_sub = lax.broadcasted_iota(jnp.int32, (64, 128), 0)
    loads[0].wait()
    loads[1].wait()
    for t in range(4):
        key = coords_ref[t, 0:1, :] * 8 + coords_ref[t, 1:2, :]
        hit = jnp.logical_and(key == sub, lane < counts_ref[0:1, t : t + 1])
        found = jnp.sum(jnp.where(hit, lane + (t * 32 + 1), 0), axis=1, keepdims=True)
        turned = jnp.sum(jnp.where(wide_lane == wide_sub, found, 0), axis=0, keepdims=True)
        slot_rows[t : t + 1, :] = jnp.where(turned == 0, live, turned - 1)
    slot_copy = pltpu.make_async_copy(slot_rows, slots, slot_sem)
    slot_copy.start()

    b1_out[...] = jnp.zeros_like(b1_out)
    part_in[rep] = jnp.zeros(part_in.shape[1:], BF16)
    pl.semaphore_wait(barrier, len(GREETED))

    even = z % 2 == y // 2
    source = jnp.logical_and(even, core == y % 2)

    def along_z(n, dz, to_core):
        return remote(
            feat_hbm.at[pl.ds(xl * 4 + to_core * 2, 2)],
            held.at[z],
            a1_send.at[n],
            a1_recv.at[z],
            (xh * 16 + ((z + dz) % 8) * 2 + to_core, rep),
        )

    def own_quarter():
        return pltpu.make_async_copy(
            feat_hbm.at[pl.ds(xl * 4 + core * 2, 2)], held.at[z], a1_recv.at[z]
        )

    def to_column(start):
        for n, dz in enumerate((2, 6, 1, 7)):
            for to_core in (0, 1):
                copy = along_z(2 * n + to_core, dz, to_core)
                copy.start() if start else copy.wait_send()
        copy = along_z(8, 0, 1 - core)
        copy.start() if start else copy.wait_send()

    pl.when(source)(lambda: (own_quarter().start(), to_column(True)) and None)
    pending.append(lambda: pl.when(source)(lambda: to_column(False)))

    def pass_along(n, dz, to, first, count):
        src = (z + dz) % 8
        piece = held.at[src, pl.ds(first, count)]
        return remote(piece, piece, a1_send.at[9 + n], a1_recv.at[src], device(0, 0, to, 0))

    relays = [(0, 2, -2, 0, 1), (1, 2, -1, 0, 2), (2, 6, 2, 1, 1), (3, 6, 1, 0, 2)]
    pending.append(
        lambda: pl.when(even)(lambda: [pass_along(*r).wait_send() for r in relays] and None)
    )

    def to_user(dz, target_xh, start):
        src = (z + dz) % 8
        user_xl = (src % 4) // 2
        mine = jnp.logical_and(user_xl == xl, xh == target_xh)
        section = xh * 2 + src // 4
        piece = held.at[src]
        place = feats.at[section, xl, core]

        @pl.when(jnp.logical_not(mine))
        def _():
            copy = remote(
                piece,
                place,
                a2_send.at[dz, target_xh],
                a2_recv.at[section],
                (target_xh * 16 + z * 2 + core, user_xl * 4 + y),
            )
            copy.start() if start else copy.wait_send()

        if start:

            @pl.when(mine)
            def _():
                pltpu.make_async_copy(piece, place, a2_recv.at[section]).start()

    def to_users(dz, start=True):
        for target_xh in (0, 1):
            to_user(dz, target_xh, start)

    def wait_piece(dz):
        src = (z + dz) % 8
        wait_bytes(held.at[src], a1_recv.at[src])

    @pl.when(even)
    def _():
        wait_piece(0)
        to_users(0)
        wait_piece(2)
        for r in relays[:2]:
            pass_along(*r).start()
        wait_piece(6)
        for r in relays[2:]:
            pass_along(*r).start()
        to_users(2)
        to_users(6)
        wait_piece(4)
        to_users(4)

    @pl.when(jnp.logical_not(even))
    def _():
        for dz in (1, 7, 3, 5):
            wait_piece(dz)
            to_users(dz)

    pending.append(lambda: pl.when(even)(lambda: [to_users(d, False) for d in (0, 2, 6, 4)] and None))
    pending.append(
        lambda: pl.when(jnp.logical_not(even))(
            lambda: [to_users(d, False) for d in (1, 7, 3, 5)] and None
        )
    )

    nearer = ((rep // 2 - z + 10) % 8) // 5
    order = [xh * 2 + nearer, 2 - xh * 2 + nearer, xh * 2 + 1 - nearer, 3 - xh * 2 - nearer]

    def pass_on(section):
        piece = feats.at[section, pl.ds(0, 2), core]
        wait_bytes(piece, a2_recv.at[section])
        launch(remote(piece, piece, a3_send.at[section], a3_recv.at[section], device(0, 0, 0, 1)))

    def complete(section):
        wait_bytes(feats.at[section, pl.ds(0, 2), 1 - core], a3_recv.at[section])

    def launch(copy):
        copy.start()
        pending.append(copy.wait_send)

    def products(r, sections, half):
        left, right = [], []
        for section in sections:
            for k in range(4):
                q = (k // 2) * 4 + half * 2 + k % 2
                left.append(tiles[slots[section, r * 8 + q]])
            right.append(feats[section, :, half].reshape(4 * 128, 128))
        return jnp.dot(
            jnp.concatenate(left, axis=1),
            jnp.concatenate(right, axis=0),
            preferred_element_type=F32,
        )

    def add_products(sections, half, first):
        for r in range(8):
            term = products(r, sections, half)
            acc[r] = term if first else acc[r] + term

    near, far = order[:2], order[2:]
    tile_copy.wait()
    slot_copy.wait()
    pass_on(near[0])
    pass_on(near[1])
    add_products(near, core, True)
    complete(near[0])
    complete(near[1])
    add_products(near, 1 - core, False)
    pass_on(far[0])
    pass_on(far[1])
    add_products(far, core, False)
    complete(far[0])
    complete(far[1])

    for i, k in enumerate((2, 1, 3, 0, 2, 1, 3, 0)):
        r = ((xl + 1 - i // 4) % 2) * 4 + (y + k) % 4
        total = acc[r] + products(r, far, 1 - core)
        if i < 7:
            part_out[r] = total.astype(BF16)
            remote(part_out.at[r], part_in.at[rep], b_send, b_recv, (row, r)).start()

    for finish in pending:
        finish()
    pending.clear()
    pending.append(lambda: wait_bytes(part_out.at[pl.ds(0, 7)], b_send))
    wait_bytes(part_in.at[pl.ds(0, 7)], b_recv)
    for s in range(8):
        total = total + part_in[s].astype(F32)

    for load in loads[3:]:
        load.wait()
    aggregated = total.astype(BF16)
    pre = jnp.dot(aggregated, weight_ref[...], preferred_element_type=F32) + bias_ref[...]
    sig = jax.nn.sigmoid(pre)
    grad = (cot_ref[...].astype(F32) * sig * (1.0 + pre * (1.0 - sig))).astype(BF16)
    weight_part = lax.dot_general(
        aggregated, grad, (((0,), (0,)), ((), ())), preferred_element_type=F32
    )
    bias_part = jnp.sum(grad.astype(F32), axis=0, keepdims=True)

    owner = plane == 0
    c1_out[0:8] = weight_part[:, 0:128].astype(BF16).reshape(8, 16, 128)
    c1_out[8:16] = weight_part[:, 128:256].astype(BF16).reshape(8, 16, 128)
    b1_out[0:1, :] = bias_part[:, 0:128]
    b1_out[1:2, :] = bias_part[:, 128:256]

    def send_bias():
        return remote(
            b1_out, b1_in.at[plane], c_send.at[3], c_recv.at[3], (z * 2 + core, 0)
        )

    @pl.when(jnp.logical_not(owner))
    def _():
        send_bias().start()

    for dx, dy in PLANE:
        p = ((x + dx) % 4) * 4 + (y + dy) % 4
        remote(
            c1_out.at[p], c1_in.at[plane], c_send.at[0], c_recv.at[0], device(dx, dy, 0, 0)
        ).start()
    c1_in[plane] = c1_out[plane]
    act_ref[...] = (pre * sig).astype(BF16)
    for finish in pending:
        finish()
    pending.clear()
    pending.append(lambda: wait_bytes(c1_out.at[pl.ds(0, 15)], c_send.at[0]))
    pending.append(lambda: pl.when(jnp.logical_not(owner))(lambda: send_bias().wait_send()))
    wait_bytes(c1_in.at[pl.ds(0, 15)], c_recv.at[0])
    core_io[core, 0:16] = jnp.sum(c1_in[...].astype(F32), axis=0)

    @pl.when(owner)
    def _():
        b1_in[0] = b1_out[...]
        wait_bytes(b1_in.at[pl.ds(0, 15)], c_recv.at[3])
        core_io[core, 16:24] = jnp.sum(b1_in[...], axis=0)

    def to_other_core():
        piece = core_io.at[core]
        return remote(piece, piece, c_send.at[4], c_recv.at[5], device(0, 0, 0, 1))

    to_other_core().start()
    wait_bytes(core_io.at[1 - core], c_recv.at[5])
    c2_in[z, 0:16] = (core_io[0, 0:16] + core_io[1, 0:16]).astype(BF16)

    def share_column(rows):
        piece = c2_in.at[z, pl.ds(0, rows)]
        for dz in ALONG_Z:
            remote(piece, piece, c_send.at[1], c_recv.at[1], device(0, 0, dz, 0)).start()
        for finish in pending:
            finish()
        wait_bytes(c2_in.at[pl.ds(0, 7), pl.ds(0, rows)], c_recv.at[1])

    @pl.when(owner)
    def _():
        both = core_io[0, 16:24] + core_io[1, 16:24]
        c2_in[z, 16:32] = jnp.concatenate([both, jnp.zeros_like(both)], axis=0).astype(BF16)
        share_column(32)
        c3_in[0, 16:24] = jnp.sum(c2_in[:, 16:32].astype(F32), axis=0)[0:8]

    pl.when(jnp.logical_not(owner))(lambda: share_column(16))
    pending.clear()

    @pending.append
    def _():
        to_other_core().wait_send()
        pl.when(owner)(lambda: wait_bytes(c2_in.at[pl.ds(0, 7)], c_send.at[1]))
        pl.when(jnp.logical_not(owner))(
            lambda: wait_bytes(c2_in.at[pl.ds(0, 7), pl.ds(0, 16)], c_send.at[1])
        )

    c3_in[plane, 0:16] = jnp.sum(c2_in[:, 0:16].astype(F32), axis=0)

    @pl.when(owner)
    def _():
        for dx, dy in PLANE:
            remote(
                c3_in.at[0], c3_in.at[0], c_send.at[2], c_recv.at[4], device(dx, dy, 0, 0)
            ).start()
        for finish in pending:
            finish()
        wait_bytes(c3_in.at[pl.ds(0, 15), pl.ds(0, 16)], c_recv.at[2])

    @pl.when(jnp.logical_not(owner))
    def _():
        piece = c3_in.at[plane, pl.ds(0, 16)]
        for dx, dy in PLANE:
            remote(piece, piece, c_send.at[2], c_recv.at[2], device(dx, dy, 0, 0)).start()
        for finish in pending:
            finish()
        wait_bytes(c3_in.at[pl.ds(0, 14), pl.ds(0, 16)], c_recv.at[2])
        wait_bytes(c3_in.at[0], c_recv.at[4])

    pending.clear()

    @pending.append
    def _():
        pl.when(owner)(lambda: wait_bytes(c3_in.at[pl.ds(0, 15)], c_send.at[2]))
        pl.when(jnp.logical_not(owner))(
            lambda: wait_bytes(c3_in.at[pl.ds(0, 15), pl.ds(0, 16)], c_send.at[2])
        )

    wg_ref[:, 0:128] = c3_in[0:8, 0:16].reshape(128, 128)
    wg_ref[:, 128:256] = c3_in[8:16, 0:16].reshape(128, 128)
    bg_ref[:, 0:128] = c3_in[0, 16:17]
    bg_ref[:, 128:256] = c3_in[0, 17:18]

    for finish in pending:
        finish()


def hand_out(act_in, wg_in, bg_in, act_ref, wg_ref, bg_ref):
    act_ref[...] = act_in[...]
    wg_ref[...] = wg_in[...]
    bg_ref[...] = bg_in[...]


def shards(features, adj_tiles, tile_coords, tile_counts, weight, out_bias, out_grad):
    vmem = pl.BlockSpec(memory_space=pltpu.VMEM)
    dma = pltpu.SemaphoreType.DMA
    outs = (
        jax.ShapeDtypeStruct((128, 256), BF16),
        jax.ShapeDtypeStruct((128, 256), F32),
        jax.ShapeDtypeStruct((1, 256), F32),
    )
    results = pl.pallas_call(
        layer_kernel,
        name="layer",
        out_shape=outs,
        in_specs=[pl.BlockSpec(memory_space=pl.ANY)] * 7,
        out_specs=(vmem, vmem, vmem),
        scratch_shapes=[
            pltpu.VMEM((1, 4), jnp.int32),
            pltpu.VMEM((4, 2, 32), jnp.int32),
            pltpu.VMEM((128, 256), BF16),
            pltpu.VMEM((1, 256), F32),
            pltpu.VMEM((128, 256), BF16),
            pltpu.VMEM((129, 128, 128), BF16),
            pltpu.VMEM((4, 128), jnp.int32),
            pltpu.SMEM((4, 128), jnp.int32),
            pltpu.VMEM((8, 2, 128, 128), BF16),
            pltpu.VMEM((4, 2, 2, 2, 128, 128), BF16),
            pltpu.VMEM((8, 128, 128), F32),
            pltpu.VMEM((8, 128, 128), BF16),
            pltpu.VMEM((8, 128, 128), BF16),
            pltpu.VMEM((16, 16, 128), BF16),
            pltpu.VMEM((16, 16, 128), BF16),
            pltpu.VMEM((8, 128), F32),
            pltpu.VMEM((16, 8, 128), F32),
            pltpu.VMEM((2, 24, 128), F32),
            pltpu.VMEM((8, 32, 128), BF16),
            pltpu.VMEM((16, 24, 128), F32),
            dma((6,)),
            dma,
            dma((16,)),
            dma((8,)),
            dma((8, 2)),
            dma((4,)),
            dma((4,)),
            dma((4,)),
            dma,
            dma,
            dma((5,)),
            dma((6,)),
        ],
        compiler_params=pltpu.CompilerParams(
            collective_id=1, has_side_effects=True, vmem_limit_bytes=60 << 20
        ),
        cost_estimate=pl.CostEstimate(
            flops=2 * 256 * 128**3, bytes_accessed=5 << 20, transcendentals=128 * 256
        ),
    )(
        tile_counts.reshape(1, 4),
        jnp.swapaxes(tile_coords[0, 0], 1, 2),
        features.reshape(8, 128, 128),
        adj_tiles.reshape(128, 128, 128),
        weight,
        out_bias.reshape(1, 256),
        out_grad,
    )
    activated, weight_grad, bias_grad = pl.pallas_call(
        hand_out,
        name="hand_out",
        out_shape=outs,
        in_specs=[vmem, vmem, vmem],
        out_specs=(vmem, vmem, vmem),
    )(*results)
    return activated, weight_grad, bias_grad.reshape(256)


def solution(mesh):
    placed = (
        P("row", None),
        P("row", "rep", None, None, None, None),
        P("row", "rep", None, None, None),
        P("row", "rep", None),
        P(),
        P(),
        P(("row", "rep"), None),
    )
    return jax.shard_map(
        shards,
        mesh=mesh,
        in_specs=placed,
        out_specs=(P(("row", "rep"), None), P(), P()),
        check_vma=False,
    )
```

```python
import functools

import jax
import jax.numpy as jnp
from jax import lax
from jax.experimental import pallas as pl
from jax.experimental.pallas import tpu as pltpu
from jax.sharding import PartitionSpec as P

MESH = pl.DeviceIdType.MESH
F32 = jnp.float32
BF16 = jnp.bfloat16

PLANE = sorted(
    [(dx, dy) for dx in range(4) for dy in range(4) if (dx, dy) != (0, 0)],
    key=lambda o: -(min(o[0], 4 - o[0]) + min(o[1], 4 - o[1])),
)
ALONG_Z = [4, 3, 5, 2, 6, 1, 7]
GREETED = [(0, 0, 0, 1)] + [(d, 0, 0, 0) for d in (2, 1, 3)] + [(0, d, 0, 0) for d in (2, 1, 3)]


def layer_kernel(
    counts_hbm,
    coords_hbm,
    feat_hbm,
    adj_hbm,
    weight_hbm,
    bias_hbm,
    cot_hbm,
    act_ref,
    wg_ref,
    bg_ref,
    counts_ref,
    coords_ref,
    weight_ref,
    bias_ref,
    cot_ref,
    tiles,
    slot_rows,
    slots,
    held,
    feats,
    acc,
    part_out,
    part_in,
    c1_out,
    c1_in,
    b1_out,
    b1_in,
    c2_in,
    c3_in,
    load_sem,
    slot_sem,
    a1_send,
    a1_recv,
    a2_send,
    a2_recv,
    a3_send,
    a3_recv,
    b_send,
    b_recv,
    c_send,
    c_recv,
):
    row = lax.axis_index("row")
    rep = lax.axis_index("rep")
    xh, z, core = row // 16, (row // 2) % 8, row % 2
    xl, y = rep // 4, rep % 4
    x = xh * 2 + xl
    plane = x * 4 + y
    live = tiles.shape[0] - 1

    def device(dx, dy, dz, dcore):
        x2, y2, z2, c2 = (x + dx) % 4, (y + dy) % 4, (z + dz) % 8, (core + dcore) % 2
        return (x2 // 2) * 16 + z2 * 2 + c2, (x2 % 2) * 4 + y2

    def remote(src, dst, send, recv, target):
        return pltpu.make_async_remote_copy(
            src_ref=src,
            dst_ref=dst,
            send_sem=send,
            recv_sem=recv,
            device_id=target,
            device_id_type=MESH,
        )

    def wait_bytes(ref, sem):
        pltpu.make_async_copy(ref, ref, sem).wait()

    barrier = pltpu.get_barrier_semaphore()
    odd_z = (z + y // 2) % 2
    other_core = (core + y) % 2

    def greet(*offset):
        pl.semaphore_signal(barrier, inc=1, device_id=device(*offset), device_id_type=MESH)

    greet(0, 0, 2 - odd_z, 0)
    greet(0, 0, 6 + odd_z, 0)

    @pl.when(other_core == 1)
    def _():
        greet(0, 0, 2 - odd_z, 1)
        greet(0, 0, 6 + odd_z, 1)

    for offset in GREETED:
        greet(*offset)

    pending = []
    loads = [
        pltpu.make_async_copy(src, dst, load_sem.at[n])
        for n, (src, dst) in enumerate(
            [
                (counts_hbm, counts_ref),
                (coords_hbm, coords_ref),
                (adj_hbm, tiles.at[pl.ds(0, live)]),
                (weight_hbm, weight_ref),
                (bias_hbm, bias_ref),
                (cot_hbm, cot_ref),
            ]
        )
    ]
    tile_copy = loads[2]
    for load in loads:
        if load is not tile_copy:
            load.start()

    tiles[live] = jnp.zeros(tiles.shape[1:], BF16)
    lane = lax.broadcasted_iota(jnp.int32, (64, 32), 1)
    sub = lax.broadcasted_iota(jnp.int32, (64, 32), 0)
    wide_lane = lax.broadcasted_iota(jnp.int32, (64, 128), 1)
    wide_sub = lax.broadcasted_iota(jnp.int32, (64, 128), 0)
    loads[0].wait()
    loads[1].wait()
    for t in range(4):
        key = coords_ref[t, 0:1, :] * 8 + coords_ref[t, 1:2, :]
        hit = jnp.logical_and(key == sub, lane < counts_ref[0:1, t : t + 1])
        found = jnp.sum(jnp.where(hit, lane + (t * 32 + 1), 0), axis=1, keepdims=True)
        turned = jnp.sum(jnp.where(wide_lane == wide_sub, found, 0), axis=0, keepdims=True)
        slot_rows[t : t + 1, :] = jnp.where(turned == 0, live, turned - 1)
    slot_copy = pltpu.make_async_copy(slot_rows, slots, slot_sem)
    slot_copy.start()

    b1_out[...] = jnp.zeros_like(b1_out)
    acc[...] = jnp.zeros_like(acc)
    part_in[rep] = jnp.zeros(part_in.shape[1:], BF16)
    pl.semaphore_wait(barrier, len(GREETED) + (1 - odd_z) * (8 - 4 * other_core))

    even = z % 2 == y // 2
    source = jnp.logical_and(even, core == y % 2)

    def along_z(n, dz, to_core, first=0, count=2):
        return remote(
            feat_hbm.at[pl.ds(xl * 4 + to_core * 2 + first, count)],
            held.at[z, pl.ds(first, count)],
            a1_send.at[n],
            a1_recv.at[z, first],
            (xh * 16 + ((z + dz) % 8) * 2 + to_core, rep),
        )

    def own_quarter():
        return pltpu.make_async_copy(
            feat_hbm.at[pl.ds(xl * 4 + core * 2, 2)], held.at[z], a1_recv.at[z, 0]
        )

    def to_column(start):
        parts = [(2, 1, 1), (6, 0, 1), (2, 0, 1), (6, 1, 1), (1, 0, 2), (7, 0, 2)]
        copies = [
            along_z(2 * n + to_core, dz, to_core, first, count)
            for n, (dz, first, count) in enumerate(parts)
            for to_core in (0, 1)
        ]
        for copy in copies + [along_z(12, 0, 1 - core)]:
            copy.start() if start else copy.wait_send()

    pl.when(source)(lambda: (own_quarter().start(), to_column(True)) and None)
    tile_copy.start()
    pending.append(lambda: pl.when(source)(lambda: to_column(False)))

    def pass_along(dz, half, start):
        src = (z + dz) % 8
        piece = held.at[src, pl.ds(half, 1)]
        side = 1 if dz == 6 else -1
        for n, far in enumerate((1, 2)):
            if far == 1 or half == (dz == 6):
                send = a1_send.at[13 + (dz // 4) * 4 + half * 2 + n]
                copy = remote(piece, piece, send, a1_recv.at[src, half], device(0, 0, side * far, 0))
                copy.start() if start else copy.wait_send()

    def to_users(dz, first, count, start=True):
        src = (z + dz) % 8
        user_xl = (src % 4) // 2
        section = xh * 2 + src // 4
        piece = held.at[src, pl.ds(first, count)]
        place = feats.at[section, xl, core, pl.ds(first, count)]

        def send(n, target_xh):
            copy = remote(
                piece,
                place,
                a2_send.at[dz, n, first],
                a2_recv.at[section],
                (target_xh * 16 + z * 2 + core, user_xl * 4 + y),
            )
            copy.start() if start else copy.wait_send()

        send(0, 1 - xh)
        pl.when(user_xl != xl)(lambda: send(1, xh))
        if start:

            @pl.when(user_xl == xl)
            def _():
                pltpu.make_async_copy(piece, place, a2_recv.at[section]).start()

    def wait_piece(dz, first, count):
        src = (z + dz) % 8
        wait_bytes(held.at[src, pl.ds(first, count)], a1_recv.at[src, first])

    even_parts = [(0, 0, 2), (2, 0, 1), (6, 1, 1), (2, 1, 1), (6, 0, 1), (4, 0, 1), (4, 1, 1)]
    odd_parts = [(1, 0, 2), (7, 0, 2), (3, 0, 1), (5, 1, 1), (3, 1, 1), (5, 0, 1)]

    @pl.when(even)
    def _():
        for dz, first, count in even_parts:
            wait_piece(dz, first, count)
            if dz in (2, 6):
                pass_along(dz, first, True)
            to_users(dz, first, count)

    @pl.when(jnp.logical_not(even))
    def _():
        for dz, first, count in odd_parts:
            wait_piece(dz, first, count)
            to_users(dz, first, count)

    def drain_even():
        for part in even_parts:
            if part[0] in (2, 6):
                pass_along(part[0], part[1], False)
            to_users(*part, start=False)

    def drain_odd():
        for part in odd_parts:
            to_users(*part, start=False)

    pending.append(lambda: pl.when(even)(drain_even))
    pending.append(lambda: pl.when(jnp.logical_not(even))(drain_odd))

    nearer = ((rep // 2 - z + 10) % 8) // 5
    def pair(turn):
        th = (turn // 2 + nearer) % 2
        return xh * 2 + th, (1 - xh) * 2 + th

    def pass_on(section, start):
        piece = feats.at[section, pl.ds(0, 2), core]
        copy = remote(
            piece, piece, a3_send.at[section], a3_recv.at[section], device(0, 0, 0, 1)
        )
        if start:
            wait_bytes(piece, a2_recv.at[section])
            copy.start()
        else:
            copy.wait_send()

    def complete(section):
        wait_bytes(feats.at[section, pl.ds(0, 2), 1 - core], a3_recv.at[section])

    def products(r, sections, half):
        left, right = [], []
        for section in sections:
            for k in range(4):
                q = (k // 2) * 4 + half * 2 + k % 2
                left.append(tiles[slots[section, r * 8 + q]])
            right.append(feats[section, :, half].reshape(4 * 128, 128))
        return jnp.dot(
            jnp.concatenate(left, axis=1),
            jnp.concatenate(right, axis=0),
            preferred_element_type=F32,
        )

    tile_copy.wait()
    slot_copy.wait()
    tile_rows = [
        ((xl + 1 - i // 4) % 2) * 4 + (y + k) % 4 for i, k in enumerate((2, 1, 3, 0, 2, 1, 3, 0))
    ]

    def add_products(turn, carry):
        sections = pair(turn)

        @pl.when(turn % 2 == 0)
        def _():
            for section in sections:
                pass_on(section, True)

        @pl.when(turn % 2 == 1)
        def _():
            for section in sections:
                complete(section)

        for r in tile_rows:
            total = acc[r] + products(r, sections, (core + turn) % 2)
            acc[r] = total
        return carry

    pending.append(lambda: [pass_on(t, False) for t in range(4)])
    lax.fori_loop(0, 3, add_products, 0)
    for section in pair(3):
        complete(section)
    for r in tile_rows:
        total = acc[r] + products(r, pair(3), 1 - core)
        if r is not tile_rows[7]:
            part_out[r] = total.astype(BF16)
            remote(part_out.at[r], part_in.at[rep], b_send, b_recv, (row, r)).start()

    for finish in pending:
        finish()
    pending.clear()
    pending.append(lambda: wait_bytes(part_out.at[pl.ds(0, 7)], b_send))
    wait_bytes(part_in.at[pl.ds(0, 7)], b_recv)
    for s in range(8):
        total = total + part_in[s].astype(F32)

    for load in loads[3:]:
        load.wait()
    aggregated = total.astype(BF16)
    pre = jnp.dot(aggregated, weight_ref[...], preferred_element_type=F32) + bias_ref[...]
    sig = jax.nn.sigmoid(pre)
    grad = (cot_ref[...].astype(F32) * sig * (1.0 + pre * (1.0 - sig))).astype(BF16)
    weight_part = lax.dot_general(
        aggregated, grad, (((0,), (0,)), ((), ())), preferred_element_type=F32
    )
    bias_part = jnp.sum(grad.astype(F32), axis=0, keepdims=True)

    first = plane == 0
    active = core == y % 2
    owner = jnp.logical_and(first, active)
    c1_out[0:8] = weight_part[:, 0:128].astype(BF16).reshape(8, 16, 128)
    c1_out[8:16] = weight_part[:, 128:256].astype(BF16).reshape(8, 16, 128)
    b1_out[0:1, :] = bias_part[:, 0:128]
    b1_out[1:2, :] = bias_part[:, 128:256]

    def send_bias():
        place = b1_in.at[plane * 2 + core]
        return remote(b1_out, place, c_send.at[3], c_recv.at[3], (z * 2, 0))

    def send_piece(dx, dy):
        x2, y2 = (x + dx) % 4, (y + dy) % 4
        target = (x2 // 2) * 16 + z * 2 + y2 % 2, (x2 % 2) * 4 + y2
        place = c1_in.at[plane * 2 + core]
        return remote(c1_out.at[x2 * 4 + y2], place, c_send.at[0], c_recv.at[0], target)

    @pl.when(jnp.logical_not(owner))
    def _():
        send_bias().start()

    for dx, dy in PLANE:
        send_piece(dx, dy).start()

    @pl.when(active)
    def _():
        c1_in[plane * 2 + core] = c1_out[plane]

    @pl.when(jnp.logical_not(active))
    def _():
        send_piece(0, 0).start()

    act_ref[...] = (pre * sig).astype(BF16)
    for finish in pending:
        finish()
    pending.clear()

    @pending.append
    def _():
        pl.when(jnp.logical_not(owner))(lambda: send_bias().wait_send())
        pl.when(active)(lambda: wait_bytes(c1_out.at[pl.ds(0, 15)], c_send.at[0]))
        pl.when(jnp.logical_not(active))(lambda: wait_bytes(c1_out, c_send.at[0]))

    pl.when(active)(lambda: wait_bytes(c1_in.at[pl.ds(0, 31)], c_recv.at[0]))

    def share_column(rows, start):
        piece = c2_in.at[z, pl.ds(0, rows)]
        for dz in ALONG_Z + [0]:
            for dcore in (0, 1):
                if dz or dcore:
                    copy = remote(
                        piece, piece, c_send.at[1], c_recv.at[1], device(0, 0, dz, dcore)
                    )
                    copy.start()

    def column_bytes(count, sem):
        pl.when(first)(lambda: wait_bytes(c2_in.at[pl.ds(0, count)], sem))
        pl.when(jnp.logical_not(first))(
            lambda: wait_bytes(c2_in.at[pl.ds(0, count), pl.ds(0, 16)], sem)
        )

    @pl.when(active)
    def _():
        c2_in[z, 0:16] = jnp.sum(c1_in[...].astype(F32), axis=0).astype(BF16)

        @pl.when(first)
        def _():
            b1_in[0] = b1_out[...]
            wait_bytes(b1_in.at[pl.ds(0, 31)], c_recv.at[3])
            both = jnp.sum(b1_in[...], axis=0)
            c2_in[z, 16:32] = jnp.concatenate([both, jnp.zeros_like(both)], axis=0).astype(BF16)
            share_column(32, True)

        pl.when(jnp.logical_not(first))(lambda: share_column(16, True))

    for finish in pending:
        finish()
    pending.clear()
    pl.when(active)(lambda: column_bytes(7, c_recv.at[1]))
    pl.when(jnp.logical_not(active))(lambda: column_bytes(8, c_recv.at[1]))

    @pl.when(first)
    def _():
        c3_in[0, 16:32] = jnp.sum(c2_in[:, 16:32].astype(F32), axis=0).astype(BF16)

    @pending.append
    def _():
        pl.when(active)(lambda: (column_bytes(8, c_send.at[1]), column_bytes(7, c_send.at[1])) and None)

    c3_in[plane, 0:16] = jnp.sum(c2_in[:, 0:16].astype(F32), axis=0).astype(BF16)

    @pl.when(first)
    def _():
        for dx, dy in PLANE:
            remote(
                c3_in.at[0], c3_in.at[0], c_send.at[2], c_recv.at[4], device(dx, dy, 0, 0)
            ).start()
        for finish in pending:
            finish()
        wait_bytes(c3_in.at[pl.ds(0, 15), pl.ds(0, 16)], c_recv.at[2])

    @pl.when(jnp.logical_not(first))
    def _():
        piece = c3_in.at[plane, pl.ds(0, 16)]
        for dx, dy in PLANE:
            remote(piece, piece, c_send.at[2], c_recv.at[2], device(dx, dy, 0, 0)).start()
        for finish in pending:
            finish()
        wait_bytes(c3_in.at[pl.ds(0, 14), pl.ds(0, 16)], c_recv.at[2])
        wait_bytes(c3_in.at[0], c_recv.at[4])

    pending.clear()

    @pending.append
    def _():
        pl.when(first)(lambda: wait_bytes(c3_in.at[pl.ds(0, 15)], c_send.at[2]))
        pl.when(jnp.logical_not(first))(
            lambda: wait_bytes(c3_in.at[pl.ds(0, 15), pl.ds(0, 16)], c_send.at[2])
        )

    wg_ref[:, 0:128] = c3_in[0:8, 0:16].astype(F32).reshape(128, 128)
    wg_ref[:, 128:256] = c3_in[8:16, 0:16].astype(F32).reshape(128, 128)
    bias_rows = c3_in[0, 16:32].astype(F32)
    bg_ref[:, 0:128] = bias_rows[0:1]
    bg_ref[:, 128:256] = bias_rows[1:2]

    for finish in pending:
        finish()


def hand_out(act_in, wg_in, bg_in, act_ref, wg_ref, bg_ref):
    act_ref[...] = act_in[...]
    wg_ref[...] = wg_in[...]
    bg_ref[...] = bg_in[...]


def shards(features, adj_tiles, tile_coords, tile_counts, weight, out_bias, out_grad):
    vmem = pl.BlockSpec(memory_space=pltpu.VMEM)
    dma = pltpu.SemaphoreType.DMA
    outs = (
        jax.ShapeDtypeStruct((128, 256), BF16),
        jax.ShapeDtypeStruct((128, 256), F32),
        jax.ShapeDtypeStruct((1, 256), F32),
    )
    results = pl.pallas_call(
        layer_kernel,
        name="layer",
        out_shape=outs,
        in_specs=[pl.BlockSpec(memory_space=pl.ANY)] * 7,
        out_specs=(vmem, vmem, vmem),
        scratch_shapes=[
            pltpu.VMEM((1, 4), jnp.int32),
            pltpu.VMEM((4, 2, 32), jnp.int32),
            pltpu.VMEM((128, 256), BF16),
            pltpu.VMEM((1, 256), F32),
            pltpu.VMEM((128, 256), BF16),
            pltpu.VMEM((129, 128, 128), BF16),
            pltpu.VMEM((4, 128), jnp.int32),
            pltpu.SMEM((4, 128), jnp.int32),
            pltpu.VMEM((8, 2, 128, 128), BF16),
            pltpu.VMEM((4, 2, 2, 2, 128, 128), BF16),
            pltpu.VMEM((8, 128, 128), F32),
            pltpu.VMEM((8, 128, 128), BF16),
            pltpu.VMEM((8, 128, 128), BF16),
            pltpu.VMEM((16, 16, 128), BF16),
            pltpu.VMEM((32, 16, 128), BF16),
            pltpu.VMEM((8, 128), F32),
            pltpu.VMEM((32, 8, 128), F32),
            pltpu.VMEM((8, 32, 128), BF16),
            pltpu.VMEM((16, 32, 128), BF16),
            dma((6,)),
            dma,
            dma((21,)),
            dma((8, 2)),
            dma((8, 2, 2)),
            dma((4,)),
            dma((4,)),
            dma((4,)),
            dma,
            dma,
            dma((5,)),
            dma((6,)),
        ],
        compiler_params=pltpu.CompilerParams(
            collective_id=1, has_side_effects=True, vmem_limit_bytes=60 << 20
        ),
        cost_estimate=pl.CostEstimate(
            flops=2 * 256 * 128**3, bytes_accessed=5 << 20, transcendentals=128 * 256
        ),
    )(
        tile_counts.reshape(1, 4),
        jnp.swapaxes(tile_coords[0, 0], 1, 2),
        features.reshape(8, 128, 128),
        adj_tiles.reshape(128, 128, 128),
        weight,
        out_bias.reshape(1, 256),
        out_grad,
    )
    activated, weight_grad, bias_grad = pl.pallas_call(
        hand_out,
        name="hand_out",
        out_shape=outs,
        in_specs=[vmem, vmem, vmem],
        out_specs=(vmem, vmem, vmem),
    )(*results)
    return activated, weight_grad, bias_grad.reshape(256)


def solution(mesh):
    placed = (
        P("row", None),
        P("row", "rep", None, None, None, None),
        P("row", "rep", None, None, None),
        P("row", "rep", None),
        P(),
        P(),
        P(("row", "rep"), None),
    )
    return jax.shard_map(
        shards,
        mesh=mesh,
        in_specs=placed,
        out_specs=(P(("row", "rep"), None), P(), P()),
        check_vma=False,
    )
```

```python
import functools

import jax
import jax.numpy as jnp
from jax import lax
from jax.experimental import pallas as pl
from jax.experimental.pallas import tpu as pltpu
from jax.sharding import PartitionSpec as P

MESH = pl.DeviceIdType.MESH
F32 = jnp.float32
BF16 = jnp.bfloat16

PLANE = sorted(
    [(dx, dy) for dx in range(4) for dy in range(4) if (dx, dy) != (0, 0)],
    key=lambda o: -(min(o[0], 4 - o[0]) + min(o[1], 4 - o[1])),
)
ALONG_Z = [4, 3, 5, 2, 6, 1, 7]
GREETED = [(0, 0, 0, 1)] + [(d, 0, 0, 0) for d in (2, 1, 3)] + [(0, d, 0, 0) for d in (2, 1, 3)]


def layer_kernel(
    counts_hbm,
    coords_hbm,
    feat_hbm,
    adj_hbm,
    weight_hbm,
    bias_hbm,
    cot_hbm,
    act_ref,
    wg_ref,
    bg_ref,
    counts_ref,
    coords_ref,
    weight_ref,
    bias_ref,
    cot_ref,
    tiles,
    slot_rows,
    slots,
    held,
    feats,
    acc,
    part_out,
    part_in,
    c1_out,
    c1_in,
    b1_out,
    b1_in,
    c2_in,
    c3_in,
    load_sem,
    slot_sem,
    a1_send,
    a1_recv,
    a2_send,
    a2_recv,
    a3_send,
    a3_recv,
    b_send,
    b_recv,
    c_send,
    c_recv,
):
    row = lax.axis_index("row")
    rep = lax.axis_index("rep")
    xh, z, core = row // 16, (row // 2) % 8, row % 2
    xl, y = rep // 4, rep % 4
    x = xh * 2 + xl
    plane = x * 4 + y
    live = tiles.shape[0] - 1

    def device(dx, dy, dz, dcore):
        x2, y2, z2, c2 = (x + dx) % 4, (y + dy) % 4, (z + dz) % 8, (core + dcore) % 2
        return (x2 // 2) * 16 + z2 * 2 + c2, (x2 % 2) * 4 + y2

    def remote(src, dst, send, recv, target):
        return pltpu.make_async_remote_copy(
            src_ref=src,
            dst_ref=dst,
            send_sem=send,
            recv_sem=recv,
            device_id=target,
            device_id_type=MESH,
        )

    def wait_bytes(ref, sem):
        pltpu.make_async_copy(ref, ref, sem).wait()

    barrier = pltpu.get_barrier_semaphore()
    odd_z = (z + y // 2) % 2
    other_core = (core + y) % 2

    def greet(*offset):
        pl.semaphore_signal(barrier, inc=1, device_id=device(*offset), device_id_type=MESH)

    greet(0, 0, 2 - odd_z, 0)
    greet(0, 0, 6 + odd_z, 0)

    @pl.when(other_core == 1)
    def _():
        greet(0, 0, 2 - odd_z, 1)
        greet(0, 0, 6 + odd_z, 1)

    for offset in GREETED:
        greet(*offset)

    pending = []
    loads = [
        pltpu.make_async_copy(src, dst, load_sem.at[n])
        for n, (src, dst) in enumerate(
            [
                (counts_hbm, counts_ref),
                (coords_hbm, coords_ref),
                (adj_hbm, tiles.at[pl.ds(0, live)]),
                (weight_hbm, weight_ref),
                (bias_hbm, bias_ref),
                (cot_hbm, cot_ref),
            ]
        )
    ]
    tile_copy = loads[2]
    for load in loads:
        if load is not tile_copy:
            load.start()

    tiles[live] = jnp.zeros(tiles.shape[1:], BF16)
    lane = lax.broadcasted_iota(jnp.int32, (64, 32), 1)
    sub = lax.broadcasted_iota(jnp.int32, (64, 32), 0)
    wide_lane = lax.broadcasted_iota(jnp.int32, (64, 128), 1)
    wide_sub = lax.broadcasted_iota(jnp.int32, (64, 128), 0)
    loads[0].wait()
    loads[1].wait()
    for t in range(4):
        key = coords_ref[t, 0:1, :] * 8 + coords_ref[t, 1:2, :]
        hit = jnp.logical_and(key == sub, lane < counts_ref[0:1, t : t + 1])
        found = jnp.sum(jnp.where(hit, lane + (t * 32 + 1), 0), axis=1, keepdims=True)
        turned = jnp.sum(jnp.where(wide_lane == wide_sub, found, 0), axis=0, keepdims=True)
        slot_rows[t : t + 1, :] = jnp.where(turned == 0, live, turned - 1)
    slot_copy = pltpu.make_async_copy(slot_rows, slots, slot_sem)
    slot_copy.start()

    b1_out[...] = jnp.zeros_like(b1_out)
    acc[...] = jnp.zeros_like(acc)
    part_in[rep] = jnp.zeros(part_in.shape[1:], BF16)
    pl.semaphore_wait(barrier, len(GREETED) + (1 - odd_z) * (8 - 4 * other_core))

    even = z % 2 == y // 2
    source = jnp.logical_and(even, core == y % 2)

    def along_z(n, dz, to_core, first=0, count=2):
        return remote(
            feat_hbm.at[pl.ds(xl * 4 + to_core * 2 + first, count)],
            held.at[z, pl.ds(first, count)],
            a1_send.at[n],
            a1_recv.at[z, first],
            (xh * 16 + ((z + dz) % 8) * 2 + to_core, rep),
        )

    def own_quarter():
        return pltpu.make_async_copy(
            feat_hbm.at[pl.ds(xl * 4 + core * 2, 2)], held.at[z], a1_recv.at[z, 0]
        )

    def to_column(start):
        parts = [(2, 1, 1), (6, 0, 1), (1, 0, 1), (7, 0, 1), (2, 0, 1), (6, 1, 1), (1, 1, 1), (7, 1, 1)]
        copies = [
            along_z(2 * n + to_core, dz, to_core, first, count)
            for n, (dz, first, count) in enumerate(parts)
            for to_core in (0, 1)
        ]
        for copy in copies + [along_z(16, 0, 1 - core)]:
            copy.start() if start else copy.wait_send()

    pl.when(source)(lambda: (own_quarter().start(), to_column(True)) and None)
    tile_copy.start()
    pending.append(lambda: pl.when(source)(lambda: to_column(False)))

    def pass_along(dz, half, start):
        src = (z + dz) % 8
        piece = held.at[src, pl.ds(half, 1)]
        side = 1 if dz == 6 else -1
        for n, far in enumerate((1, 2)):
            if far == 1 or half == (dz == 6):
                send = a1_send.at[17 + (dz // 4) * 4 + half * 2 + n]
                copy = remote(piece, piece, send, a1_recv.at[src, half], device(0, 0, side * far, 0))
                copy.start() if start else copy.wait_send()

    def to_users(dz, first, count, start=True):
        src = (z + dz) % 8
        user_xl = (src % 4) // 2
        section = xh * 2 + src // 4
        piece = held.at[src, pl.ds(first, count)]
        place = feats.at[section, xl, core, pl.ds(first, count)]

        def send(n, target_xh):
            copy = remote(
                piece,
                place,
                a2_send.at[dz, n, first],
                a2_recv.at[section],
                (target_xh * 16 + z * 2 + core, user_xl * 4 + y),
            )
            copy.start() if start else copy.wait_send()

        send(0, 1 - xh)
        pl.when(user_xl != xl)(lambda: send(1, xh))
        if start:

            @pl.when(user_xl == xl)
            def _():
                pltpu.make_async_copy(piece, place, a2_recv.at[section]).start()

    def wait_piece(dz, first, count):
        src = (z + dz) % 8
        wait_bytes(held.at[src, pl.ds(first, count)], a1_recv.at[src, first])

    even_parts = [(0, 0, 2), (2, 0, 1), (6, 1, 1), (2, 1, 1), (6, 0, 1), (4, 0, 1), (4, 1, 1)]
    odd_parts = [(1, 0, 1), (7, 0, 1), (1, 1, 1), (7, 1, 1), (3, 0, 1), (5, 1, 1), (3, 1, 1), (5, 0, 1)]

    @pl.when(even)
    def _():
        for dz, first, count in even_parts:
            wait_piece(dz, first, count)
            if dz in (2, 6):
                pass_along(dz, first, True)
            to_users(dz, first, count)

    @pl.when(jnp.logical_not(even))
    def _():
        for dz, first, count in odd_parts:
            wait_piece(dz, first, count)
            to_users(dz, first, count)

    def drain_even():
        for part in even_parts:
            if part[0] in (2, 6):
                pass_along(part[0], part[1], False)
            to_users(*part, start=False)

    def drain_odd():
        for part in odd_parts:
            to_users(*part, start=False)

    pending.append(lambda: pl.when(even)(drain_even))
    pending.append(lambda: pl.when(jnp.logical_not(even))(drain_odd))

    nearer = ((rep // 2 - z + 10) % 8) // 5
    def pair(turn):
        th = (turn // 2 + nearer) % 2
        return xh * 2 + th, (1 - xh) * 2 + th

    def pass_on(section, start):
        piece = feats.at[section, pl.ds(0, 2), core]
        copy = remote(
            piece, piece, a3_send.at[section], a3_recv.at[section], device(0, 0, 0, 1)
        )
        if start:
            wait_bytes(piece, a2_recv.at[section])
            copy.start()
        else:
            copy.wait_send()

    def complete(section):
        wait_bytes(feats.at[section, pl.ds(0, 2), 1 - core], a3_recv.at[section])

    def products(r, sections, half):
        left, right = [], []
        for section in sections:
            for k in range(4):
                q = (k // 2) * 4 + half * 2 + k % 2
                left.append(tiles[slots[section, r * 8 + q]])
            right.append(feats[section, :, half].reshape(4 * 128, 128))
        return jnp.dot(
            jnp.concatenate(left, axis=1),
            jnp.concatenate(right, axis=0),
            preferred_element_type=F32,
        )

    tile_copy.wait()
    slot_copy.wait()
    tile_rows = [
        ((xl + 1 - i // 4) % 2) * 4 + (y + k) % 4 for i, k in enumerate((2, 1, 3, 0, 2, 1, 3, 0))
    ]

    def add_products(turn, carry):
        sections = pair(turn)

        @pl.when(turn % 2 == 0)
        def _():
            for section in sections:
                pass_on(section, True)

        @pl.when(turn % 2 == 1)
        def _():
            for section in sections:
                complete(section)

        for r in tile_rows:
            total = acc[r] + products(r, sections, (core + turn) % 2)
            acc[r] = total
        return carry

    pending.append(lambda: [pass_on(t, False) for t in range(4)])
    lax.fori_loop(0, 3, add_products, 0)
    for section in pair(3):
        complete(section)
    for r in tile_rows:
        total = acc[r] + products(r, pair(3), 1 - core)
        if r is not tile_rows[7]:
            part_out[r] = total.astype(BF16)
            remote(part_out.at[r], part_in.at[rep], b_send, b_recv, (row, r)).start()

    for finish in pending:
        finish()
    pending.clear()
    pending.append(lambda: wait_bytes(part_out.at[pl.ds(0, 7)], b_send))
    wait_bytes(part_in.at[pl.ds(0, 7)], b_recv)
    for s in range(8):
        total = total + part_in[s].astype(F32)

    for load in loads[3:]:
        load.wait()
    aggregated = total.astype(BF16)
    pre = jnp.dot(aggregated, weight_ref[...], preferred_element_type=F32) + bias_ref[...]
    sig = jax.nn.sigmoid(pre)
    grad = (cot_ref[...].astype(F32) * sig * (1.0 + pre * (1.0 - sig))).astype(BF16)
    weight_part = lax.dot_general(
        aggregated, grad, (((0,), (0,)), ((), ())), preferred_element_type=F32
    )
    bias_part = jnp.sum(grad.astype(F32), axis=0, keepdims=True)

    first = plane == 0
    active = core == y % 2
    owner = jnp.logical_and(first, active)
    c1_out[0:8] = weight_part[:, 0:128].astype(BF16).reshape(8, 16, 128)
    c1_out[8:16] = weight_part[:, 128:256].astype(BF16).reshape(8, 16, 128)
    b1_out[0:1, :] = bias_part[:, 0:128]
    b1_out[1:2, :] = bias_part[:, 128:256]

    def send_bias():
        place = b1_in.at[plane * 2 + core]
        return remote(b1_out, place, c_send.at[3], c_recv.at[3], (z * 2, 0))

    def send_piece(dx, dy):
        x2, y2 = (x + dx) % 4, (y + dy) % 4
        target = (x2 // 2) * 16 + z * 2 + y2 % 2, (x2 % 2) * 4 + y2
        place = c1_in.at[plane * 2 + core]
        return remote(c1_out.at[x2 * 4 + y2], place, c_send.at[0], c_recv.at[0], target)

    @pl.when(jnp.logical_not(owner))
    def _():
        send_bias().start()

    for dx, dy in PLANE:
        send_piece(dx, dy).start()

    @pl.when(active)
    def _():
        c1_in[plane * 2 + core] = c1_out[plane]

    @pl.when(jnp.logical_not(active))
    def _():
        send_piece(0, 0).start()

    act_ref[...] = (pre * sig).astype(BF16)
    for finish in pending:
        finish()
    pending.clear()

    @pending.append
    def _():
        pl.when(jnp.logical_not(owner))(lambda: send_bias().wait_send())
        pl.when(active)(lambda: wait_bytes(c1_out.at[pl.ds(0, 15)], c_send.at[0]))
        pl.when(jnp.logical_not(active))(lambda: wait_bytes(c1_out, c_send.at[0]))

    pl.when(active)(lambda: wait_bytes(c1_in.at[pl.ds(0, 31)], c_recv.at[0]))

    def share_column(rows, start):
        piece = c2_in.at[z, pl.ds(0, rows)]
        for dz in ALONG_Z + [0]:
            for dcore in (0, 1):
                if dz or dcore:
                    copy = remote(
                        piece, piece, c_send.at[1], c_recv.at[1], device(0, 0, dz, dcore)
                    )
                    copy.start()

    def column_bytes(count, sem):
        pl.when(first)(lambda: wait_bytes(c2_in.at[pl.ds(0, count)], sem))
        pl.when(jnp.logical_not(first))(
            lambda: wait_bytes(c2_in.at[pl.ds(0, count), pl.ds(0, 16)], sem)
        )

    @pl.when(active)
    def _():
        c2_in[z, 0:16] = jnp.sum(c1_in[...].astype(F32), axis=0).astype(BF16)

        @pl.when(first)
        def _():
            b1_in[0] = b1_out[...]
            wait_bytes(b1_in.at[pl.ds(0, 31)], c_recv.at[3])
            both = jnp.sum(b1_in[...], axis=0)
            c2_in[z, 16:32] = jnp.concatenate([both, jnp.zeros_like(both)], axis=0).astype(BF16)
            share_column(32, True)

        pl.when(jnp.logical_not(first))(lambda: share_column(16, True))

    for finish in pending:
        finish()
    pending.clear()
    pl.when(active)(lambda: column_bytes(7, c_recv.at[1]))
    pl.when(jnp.logical_not(active))(lambda: column_bytes(8, c_recv.at[1]))

    @pl.when(first)
    def _():
        c3_in[0, 16:32] = jnp.sum(c2_in[:, 16:32].astype(F32), axis=0).astype(BF16)

    @pending.append
    def _():
        pl.when(active)(lambda: (column_bytes(8, c_send.at[1]), column_bytes(7, c_send.at[1])) and None)

    c3_in[plane, 0:16] = jnp.sum(c2_in[:, 0:16].astype(F32), axis=0).astype(BF16)

    @pl.when(first)
    def _():
        for dx, dy in PLANE:
            remote(
                c3_in.at[0], c3_in.at[0], c_send.at[2], c_recv.at[4], device(dx, dy, 0, 0)
            ).start()
        for finish in pending:
            finish()
        wait_bytes(c3_in.at[pl.ds(0, 15), pl.ds(0, 16)], c_recv.at[2])

    @pl.when(jnp.logical_not(first))
    def _():
        piece = c3_in.at[plane, pl.ds(0, 16)]
        for dx, dy in PLANE:
            remote(piece, piece, c_send.at[2], c_recv.at[2], device(dx, dy, 0, 0)).start()
        for finish in pending:
            finish()
        wait_bytes(c3_in.at[pl.ds(0, 14), pl.ds(0, 16)], c_recv.at[2])
        wait_bytes(c3_in.at[0], c_recv.at[4])

    pending.clear()

    @pending.append
    def _():
        pl.when(first)(lambda: wait_bytes(c3_in.at[pl.ds(0, 15)], c_send.at[2]))
        pl.when(jnp.logical_not(first))(
            lambda: wait_bytes(c3_in.at[pl.ds(0, 15), pl.ds(0, 16)], c_send.at[2])
        )

    wg_ref[:, 0:128] = c3_in[0:8, 0:16].astype(F32).reshape(128, 128)
    wg_ref[:, 128:256] = c3_in[8:16, 0:16].astype(F32).reshape(128, 128)
    bias_rows = c3_in[0, 16:32].astype(F32)
    bg_ref[:, 0:128] = bias_rows[0:1]
    bg_ref[:, 128:256] = bias_rows[1:2]

    for finish in pending:
        finish()


def hand_out(act_in, wg_in, bg_in, act_ref, wg_ref, bg_ref):
    act_ref[...] = act_in[...]
    wg_ref[...] = wg_in[...]
    bg_ref[...] = bg_in[...]


def shards(features, adj_tiles, tile_coords, tile_counts, weight, out_bias, out_grad):
    vmem = pl.BlockSpec(memory_space=pltpu.VMEM)
    dma = pltpu.SemaphoreType.DMA
    outs = (
        jax.ShapeDtypeStruct((128, 256), BF16),
        jax.ShapeDtypeStruct((128, 256), F32),
        jax.ShapeDtypeStruct((1, 256), F32),
    )
    results = pl.pallas_call(
        layer_kernel,
        name="layer",
        out_shape=outs,
        in_specs=[pl.BlockSpec(memory_space=pl.ANY)] * 7,
        out_specs=(vmem, vmem, vmem),
        scratch_shapes=[
            pltpu.VMEM((1, 4), jnp.int32),
            pltpu.VMEM((4, 2, 32), jnp.int32),
            pltpu.VMEM((128, 256), BF16),
            pltpu.VMEM((1, 256), F32),
            pltpu.VMEM((128, 256), BF16),
            pltpu.VMEM((129, 128, 128), BF16),
            pltpu.VMEM((4, 128), jnp.int32),
            pltpu.SMEM((4, 128), jnp.int32),
            pltpu.VMEM((8, 2, 128, 128), BF16),
            pltpu.VMEM((4, 2, 2, 2, 128, 128), BF16),
            pltpu.VMEM((8, 128, 128), F32),
            pltpu.VMEM((8, 128, 128), BF16),
            pltpu.VMEM((8, 128, 128), BF16),
            pltpu.VMEM((16, 16, 128), BF16),
            pltpu.VMEM((32, 16, 128), BF16),
            pltpu.VMEM((8, 128), F32),
            pltpu.VMEM((32, 8, 128), F32),
            pltpu.VMEM((8, 32, 128), BF16),
            pltpu.VMEM((16, 32, 128), BF16),
            dma((6,)),
            dma,
            dma((25,)),
            dma((8, 2)),
            dma((8, 2, 2)),
            dma((4,)),
            dma((4,)),
            dma((4,)),
            dma,
            dma,
            dma((5,)),
            dma((6,)),
        ],
        compiler_params=pltpu.CompilerParams(
            collective_id=1, has_side_effects=True, vmem_limit_bytes=60 << 20
        ),
        cost_estimate=pl.CostEstimate(
            flops=2 * 256 * 128**3, bytes_accessed=5 << 20, transcendentals=128 * 256
        ),
    )(
        tile_counts.reshape(1, 4),
        jnp.swapaxes(tile_coords[0, 0], 1, 2),
        features.reshape(8, 128, 128),
        adj_tiles.reshape(128, 128, 128),
        weight,
        out_bias.reshape(1, 256),
        out_grad,
    )
    activated, weight_grad, bias_grad = pl.pallas_call(
        hand_out,
        name="hand_out",
        out_shape=outs,
        in_specs=[vmem, vmem, vmem],
        out_specs=(vmem, vmem, vmem),
    )(*results)
    return activated, weight_grad, bias_grad.reshape(256)


def solution(mesh):
    placed = (
        P("row", None),
        P("row", "rep", None, None, None, None),
        P("row", "rep", None, None, None),
        P("row", "rep", None),
        P(),
        P(),
        P(("row", "rep"), None),
    )
    return jax.shard_map(
        shards,
        mesh=mesh,
        in_specs=placed,
        out_specs=(P(("row", "rep"), None), P(), P()),
        check_vma=False,
    )
```

```python
import functools

import jax
import jax.numpy as jnp
from jax import lax
from jax.experimental import pallas as pl
from jax.experimental.pallas import tpu as pltpu
from jax.sharding import PartitionSpec as P

MESH = pl.DeviceIdType.MESH
F32 = jnp.float32
BF16 = jnp.bfloat16

PLANE = sorted(
    [(dx, dy) for dx in range(4) for dy in range(4) if (dx, dy) != (0, 0)],
    key=lambda o: -(min(o[0], 4 - o[0]) + min(o[1], 4 - o[1])),
)
ALONG_Z = [4, 3, 5, 2, 6, 1, 7]
GREETED = [(0, 0, 0, 1)] + [(d, 0, 0, 0) for d in (2, 1, 3)] + [(0, d, 0, 0) for d in (2, 1, 3)]


def layer_kernel(
    counts_hbm,
    coords_hbm,
    feat_hbm,
    adj_hbm,
    weight_hbm,
    bias_hbm,
    cot_hbm,
    act_ref,
    wg_ref,
    counts_ref,
    coords_ref,
    weight_ref,
    bias_ref,
    cot_ref,
    tiles,
    slot_rows,
    slots,
    held,
    feats,
    acc,
    part_out,
    part_in,
    c1_out,
    c1_in,
    b1_out,
    b1_in,
    c2_in,
    c3_in,
    load_sem,
    slot_sem,
    a1_send,
    a1_recv,
    a2_send,
    a2_recv,
    a3_send,
    a3_recv,
    b_send,
    b_recv,
    c_send,
    c_recv,
):
    row = lax.axis_index("row")
    rep = lax.axis_index("rep")
    xh, z, core = row // 16, (row // 2) % 8, row % 2
    xl, y = rep // 4, rep % 4
    x = xh * 2 + xl
    plane = x * 4 + y
    live = tiles.shape[0] - 1

    def device(dx, dy, dz, dcore):
        x2, y2, z2, c2 = (x + dx) % 4, (y + dy) % 4, (z + dz) % 8, (core + dcore) % 2
        return (x2 // 2) * 16 + z2 * 2 + c2, (x2 % 2) * 4 + y2

    def remote(src, dst, send, recv, target):
        return pltpu.make_async_remote_copy(
            src_ref=src,
            dst_ref=dst,
            send_sem=send,
            recv_sem=recv,
            device_id=target,
            device_id_type=MESH,
        )

    def wait_bytes(ref, sem):
        pltpu.make_async_copy(ref, ref, sem).wait()

    barrier = pltpu.get_barrier_semaphore()
    odd_z = (z + y // 2) % 2
    other_core = (core + y) % 2

    def greet(*offset):
        pl.semaphore_signal(barrier, inc=1, device_id=device(*offset), device_id_type=MESH)

    greet(0, 0, 2 - odd_z, 0)
    greet(0, 0, 6 + odd_z, 0)

    @pl.when(other_core == 1)
    def _():
        greet(0, 0, 2 - odd_z, 1)
        greet(0, 0, 6 + odd_z, 1)

    for offset in GREETED:
        greet(*offset)

    pending = []
    loads = [
        pltpu.make_async_copy(src, dst, load_sem.at[n])
        for n, (src, dst) in enumerate(
            [
                (counts_hbm, counts_ref),
                (coords_hbm, coords_ref),
                (adj_hbm, tiles.at[pl.ds(0, live)]),
                (weight_hbm, weight_ref),
                (bias_hbm, bias_ref),
                (cot_hbm, cot_ref),
            ]
        )
    ]
    tile_copy = loads[2]
    for load in loads:
        if load is not tile_copy:
            load.start()

    tiles[live] = jnp.zeros(tiles.shape[1:], BF16)
    lane = lax.broadcasted_iota(jnp.int32, (64, 32), 1)
    sub = lax.broadcasted_iota(jnp.int32, (64, 32), 0)
    wide_lane = lax.broadcasted_iota(jnp.int32, (64, 128), 1)
    wide_sub = lax.broadcasted_iota(jnp.int32, (64, 128), 0)
    loads[0].wait()
    loads[1].wait()
    for t in range(4):
        key = coords_ref[t, 0:1, :] * 8 + coords_ref[t, 1:2, :]
        hit = jnp.logical_and(key == sub, lane < counts_ref[0:1, t : t + 1])
        found = jnp.sum(jnp.where(hit, lane + (t * 32 + 1), 0), axis=1, keepdims=True)
        turned = jnp.sum(jnp.where(wide_lane == wide_sub, found, 0), axis=0, keepdims=True)
        slot_rows[t : t + 1, :] = jnp.where(turned == 0, live, turned - 1)
    slot_copy = pltpu.make_async_copy(slot_rows, slots, slot_sem)
    slot_copy.start()

    b1_out[...] = jnp.zeros_like(b1_out)
    acc[...] = jnp.zeros_like(acc)
    part_in[rep] = jnp.zeros(part_in.shape[1:], BF16)
    pl.semaphore_wait(barrier, len(GREETED) + (1 - odd_z) * (8 - 4 * other_core))

    even = z % 2 == y // 2
    source = jnp.logical_and(even, core == y % 2)

    def along_z(n, dz, to_core, first=0, count=2):
        return remote(
            feat_hbm.at[pl.ds(xl * 4 + to_core * 2 + first, count)],
            held.at[z, pl.ds(first, count)],
            a1_send.at[n],
            a1_recv.at[z, first],
            (xh * 16 + ((z + dz) % 8) * 2 + to_core, rep),
        )

    def own_quarter():
        return pltpu.make_async_copy(
            feat_hbm.at[pl.ds(xl * 4 + core * 2, 2)], held.at[z], a1_recv.at[z, 0]
        )

    def to_column(start):
        parts = [(2, 1, 1), (6, 0, 1), (1, 0, 1), (7, 0, 1), (2, 0, 1), (6, 1, 1), (1, 1, 1), (7, 1, 1)]
        copies = [
            along_z(2 * n + to_core, dz, to_core, first, count)
            for n, (dz, first, count) in enumerate(parts)
            for to_core in (0, 1)
        ]
        for copy in copies + [along_z(16, 0, 1 - core)]:
            copy.start() if start else copy.wait_send()

    pl.when(source)(lambda: (own_quarter().start(), to_column(True)) and None)
    tile_copy.start()
    pending.append(lambda: pl.when(source)(lambda: to_column(False)))

    def pass_along(dz, half, start):
        src = (z + dz) % 8
        piece = held.at[src, pl.ds(half, 1)]
        side = 1 if dz == 6 else -1
        for n, far in enumerate((1, 2)):
            if far == 1 or half == (dz == 6):
                send = a1_send.at[17 + (dz // 4) * 4 + half * 2 + n]
                copy = remote(piece, piece, send, a1_recv.at[src, half], device(0, 0, side * far, 0))
                copy.start() if start else copy.wait_send()

    def to_users(dz, first, count, start=True):
        src = (z + dz) % 8
        user_xl = (src % 4) // 2
        section = xh * 2 + src // 4
        piece = held.at[src, pl.ds(first, count)]
        place = feats.at[section, xl, core, pl.ds(first, count)]

        def send(n, target_xh):
            copy = remote(
                piece,
                place,
                a2_send.at[dz, n, first],
                a2_recv.at[section],
                (target_xh * 16 + z * 2 + core, user_xl * 4 + y),
            )
            copy.start() if start else copy.wait_send()

        send(0, 1 - xh)
        pl.when(user_xl != xl)(lambda: send(1, xh))
        if start:

            @pl.when(user_xl == xl)
            def _():
                pltpu.make_async_copy(piece, place, a2_recv.at[section]).start()

    def wait_piece(dz, first, count):
        src = (z + dz) % 8
        wait_bytes(held.at[src, pl.ds(first, count)], a1_recv.at[src, first])

    even_parts = [(0, 0, 2), (2, 0, 1), (6, 1, 1), (2, 1, 1), (6, 0, 1), (4, 0, 1), (4, 1, 1)]
    odd_parts = [(1, 0, 1), (7, 0, 1), (1, 1, 1), (7, 1, 1), (3, 0, 1), (5, 1, 1), (3, 1, 1), (5, 0, 1)]

    @pl.when(even)
    def _():
        for dz, first, count in even_parts:
            wait_piece(dz, first, count)
            if dz in (2, 6):
                pass_along(dz, first, True)
            to_users(dz, first, count)

    @pl.when(jnp.logical_not(even))
    def _():
        for dz, first, count in odd_parts:
            wait_piece(dz, first, count)
            to_users(dz, first, count)

    def drain_even():
        for part in even_parts:
            if part[0] in (2, 6):
                pass_along(part[0], part[1], False)
            to_users(*part, start=False)

    def drain_odd():
        for part in odd_parts:
            to_users(*part, start=False)

    pending.append(lambda: pl.when(even)(drain_even))
    pending.append(lambda: pl.when(jnp.logical_not(even))(drain_odd))

    nearer = ((rep // 2 - z + 10) % 8) // 5
    def pair(turn):
        th = (turn // 2 + nearer) % 2
        return xh * 2 + th, (1 - xh) * 2 + th

    def pass_on(section, start):
        piece = feats.at[section, pl.ds(0, 2), core]
        copy = remote(
            piece, piece, a3_send.at[section], a3_recv.at[section], device(0, 0, 0, 1)
        )
        if start:
            wait_bytes(piece, a2_recv.at[section])
            copy.start()
        else:
            copy.wait_send()

    def complete(section):
        wait_bytes(feats.at[section, pl.ds(0, 2), 1 - core], a3_recv.at[section])

    def products(r, sections, half):
        left, right = [], []
        for section in sections:
            for k in range(4):
                q = (k // 2) * 4 + half * 2 + k % 2
                left.append(tiles[slots[section, r * 8 + q]])
            right.append(feats[section, :, half].reshape(4 * 128, 128))
        return jnp.dot(
            jnp.concatenate(left, axis=1),
            jnp.concatenate(right, axis=0),
            preferred_element_type=F32,
        )

    tile_copy.wait()
    slot_copy.wait()
    tile_rows = [
        ((xl + 1 - i // 4) % 2) * 4 + (y + k) % 4 for i, k in enumerate((2, 1, 3, 0, 2, 1, 3, 0))
    ]

    def add_products(turn, carry):
        sections = pair(turn)

        @pl.when(turn % 2 == 0)
        def _():
            for section in sections:
                pass_on(section, True)

        @pl.when(turn % 2 == 1)
        def _():
            for section in sections:
                complete(section)

        for r in tile_rows:
            total = acc[r] + products(r, sections, (core + turn) % 2)
            acc[r] = total
            part_out[r] = total.astype(BF16)
        return carry

    pending.append(lambda: [pass_on(t, False) for t in range(4)])
    lax.fori_loop(0, 4, add_products, 0)
    for r in tile_rows[:7]:
        remote(part_out.at[r], part_in.at[rep], b_send, b_recv, (row, r)).start()
    total = acc[rep]

    for finish in pending:
        finish()
    pending.clear()
    pending.append(lambda: wait_bytes(part_out.at[pl.ds(0, 7)], b_send))
    wait_bytes(part_in.at[pl.ds(0, 7)], b_recv)
    for s in range(8):
        total = total + part_in[s].astype(F32)

    for load in loads[3:]:
        load.wait()
    aggregated = total.astype(BF16)
    pre = jnp.dot(aggregated, weight_ref[...], preferred_element_type=F32) + bias_ref[...]
    sig = jax.nn.sigmoid(pre)
    grad = (cot_ref[...].astype(F32) * sig * (1.0 + pre * (1.0 - sig))).astype(BF16)
    weight_part = lax.dot_general(
        aggregated, grad, (((0,), (0,)), ((), ())), preferred_element_type=F32
    )
    bias_part = jnp.sum(grad.astype(F32), axis=0, keepdims=True)

    first = plane == 0
    active = core == y % 2
    owner = jnp.logical_and(first, active)
    c1_out[0:8] = weight_part[:, 0:128].astype(BF16).reshape(8, 16, 128)
    c1_out[8:16] = weight_part[:, 128:256].astype(BF16).reshape(8, 16, 128)
    b1_out[0:1, :] = bias_part[:, 0:128]
    b1_out[1:2, :] = bias_part[:, 128:256]

    def send_bias():
        place = b1_in.at[plane * 2 + core]
        return remote(b1_out, place, c_send.at[3], c_recv.at[3], (z * 2, 0))

    def send_piece(dx, dy):
        x2, y2 = (x + dx) % 4, (y + dy) % 4
        target = (x2 // 2) * 16 + z * 2 + y2 % 2, (x2 % 2) * 4 + y2
        place = c1_in.at[plane * 2 + core]
        return remote(c1_out.at[x2 * 4 + y2], place, c_send.at[0], c_recv.at[0], target)

    @pl.when(jnp.logical_not(owner))
    def _():
        send_bias().start()

    for dx, dy in PLANE:
        send_piece(dx, dy).start()

    @pl.when(active)
    def _():
        c1_in[plane * 2 + core] = c1_out[plane]

    @pl.when(jnp.logical_not(active))
    def _():
        send_piece(0, 0).start()

    act_ref[...] = (pre * sig).astype(BF16)
    for finish in pending:
        finish()
    pending.clear()

    @pending.append
    def _():
        pl.when(jnp.logical_not(owner))(lambda: send_bias().wait_send())
        pl.when(active)(lambda: wait_bytes(c1_out.at[pl.ds(0, 15)], c_send.at[0]))
        pl.when(jnp.logical_not(active))(lambda: wait_bytes(c1_out, c_send.at[0]))

    pl.when(active)(lambda: wait_bytes(c1_in.at[pl.ds(0, 31)], c_recv.at[0]))

    def share_column(rows, start):
        piece = c2_in.at[z, pl.ds(0, rows)]
        for dz in ALONG_Z + [0]:
            for dcore in (0, 1):
                if dz or dcore:
                    copy = remote(
                        piece, piece, c_send.at[1], c_recv.at[1], device(0, 0, dz, dcore)
                    )
                    copy.start()

    def column_bytes(count, sem):
        pl.when(first)(lambda: wait_bytes(c2_in.at[pl.ds(0, count)], sem))
        pl.when(jnp.logical_not(first))(
            lambda: wait_bytes(c2_in.at[pl.ds(0, count), pl.ds(0, 16)], sem)
        )

    @pl.when(active)
    def _():
        c2_in[z, 0:16] = jnp.sum(c1_in[...].astype(F32), axis=0).astype(BF16)

        @pl.when(first)
        def _():
            b1_in[0] = b1_out[...]
            wait_bytes(b1_in.at[pl.ds(0, 31)], c_recv.at[3])
            both = jnp.sum(b1_in[...], axis=0)
            c2_in[z, 16:32] = jnp.concatenate([both, jnp.zeros_like(both)], axis=0).astype(BF16)
            share_column(32, True)

        pl.when(jnp.logical_not(first))(lambda: share_column(16, True))

    for finish in pending:
        finish()
    pending.clear()
    pl.when(active)(lambda: column_bytes(7, c_recv.at[1]))
    pl.when(jnp.logical_not(active))(lambda: column_bytes(8, c_recv.at[1]))

    @pl.when(first)
    def _():
        c3_in[0, 16:32] = jnp.sum(c2_in[:, 16:32].astype(F32), axis=0).astype(BF16)

    @pending.append
    def _():
        pl.when(active)(lambda: (column_bytes(8, c_send.at[1]), column_bytes(7, c_send.at[1])) and None)

    c3_in[plane, 0:16] = jnp.sum(c2_in[:, 0:16].astype(F32), axis=0).astype(BF16)

    @pl.when(first)
    def _():
        for dx, dy in PLANE:
            remote(
                c3_in.at[0], c3_in.at[0], c_send.at[2], c_recv.at[4], device(dx, dy, 0, 0)
            ).start()
        for finish in pending:
            finish()
        wait_bytes(c3_in.at[pl.ds(0, 15), pl.ds(0, 16)], c_recv.at[2])

    @pl.when(jnp.logical_not(first))
    def _():
        piece = c3_in.at[plane, pl.ds(0, 16)]
        for dx, dy in PLANE:
            remote(piece, piece, c_send.at[2], c_recv.at[2], device(dx, dy, 0, 0)).start()
        for finish in pending:
            finish()
        wait_bytes(c3_in.at[pl.ds(0, 14), pl.ds(0, 16)], c_recv.at[2])
        wait_bytes(c3_in.at[0], c_recv.at[4])

    pending.clear()

    @pending.append
    def _():
        pl.when(first)(lambda: wait_bytes(c3_in.at[pl.ds(0, 15)], c_send.at[2]))
        pl.when(jnp.logical_not(first))(
            lambda: wait_bytes(c3_in.at[pl.ds(0, 15), pl.ds(0, 16)], c_send.at[2])
        )

    wg_ref[...] = c3_in[...]

    for finish in pending:
        finish()


def hand_out(act_in, pieces, act_ref, wg_ref, bg_ref):
    act_ref[...] = act_in[...]
    wg_ref[:, 0:128] = pieces[0:8, 0:16].astype(F32).reshape(128, 128)
    wg_ref[:, 128:256] = pieces[8:16, 0:16].astype(F32).reshape(128, 128)
    bias_rows = pieces[0, 16:32].astype(F32)
    bg_ref[:, 0:128] = bias_rows[0:1]
    bg_ref[:, 128:256] = bias_rows[1:2]


def shards(features, adj_tiles, tile_coords, tile_counts, weight, out_bias, out_grad):
    vmem = pl.BlockSpec(memory_space=pltpu.VMEM)
    dma = pltpu.SemaphoreType.DMA
    outs = (
        jax.ShapeDtypeStruct((128, 256), BF16),
        jax.ShapeDtypeStruct((128, 256), F32),
        jax.ShapeDtypeStruct((1, 256), F32),
    )
    results = pl.pallas_call(
        layer_kernel,
        name="layer",
        out_shape=(outs[0], jax.ShapeDtypeStruct((16, 32, 128), BF16)),
        in_specs=[pl.BlockSpec(memory_space=pl.ANY)] * 7,
        out_specs=(vmem, vmem),
        scratch_shapes=[
            pltpu.VMEM((1, 4), jnp.int32),
            pltpu.VMEM((4, 2, 32), jnp.int32),
            pltpu.VMEM((128, 256), BF16),
            pltpu.VMEM((1, 256), F32),
            pltpu.VMEM((128, 256), BF16),
            pltpu.VMEM((129, 128, 128), BF16),
            pltpu.VMEM((4, 128), jnp.int32),
            pltpu.SMEM((4, 128), jnp.int32),
            pltpu.VMEM((8, 2, 128, 128), BF16),
            pltpu.VMEM((4, 2, 2, 2, 128, 128), BF16),
            pltpu.VMEM((8, 128, 128), F32),
            pltpu.VMEM((8, 128, 128), BF16),
            pltpu.VMEM((8, 128, 128), BF16),
            pltpu.VMEM((16, 16, 128), BF16),
            pltpu.VMEM((32, 16, 128), BF16),
            pltpu.VMEM((8, 128), F32),
            pltpu.VMEM((32, 8, 128), F32),
            pltpu.VMEM((8, 32, 128), BF16),
            pltpu.VMEM((16, 32, 128), BF16),
            dma((6,)),
            dma,
            dma((25,)),
            dma((8, 2)),
            dma((8, 2, 2)),
            dma((4,)),
            dma((4,)),
            dma((4,)),
            dma,
            dma,
            dma((5,)),
            dma((6,)),
        ],
        compiler_params=pltpu.CompilerParams(
            collective_id=1, has_side_effects=True, vmem_limit_bytes=60 << 20
        ),
        cost_estimate=pl.CostEstimate(
            flops=2 * 256 * 128**3, bytes_accessed=5 << 20, transcendentals=128 * 256
        ),
    )(
        tile_counts.reshape(1, 4),
        jnp.swapaxes(tile_coords[0, 0], 1, 2),
        features.reshape(8, 128, 128),
        adj_tiles.reshape(128, 128, 128),
        weight,
        out_bias.reshape(1, 256),
        out_grad,
    )
    activated, weight_grad, bias_grad = pl.pallas_call(
        hand_out,
        name="hand_out",
        out_shape=outs,
        in_specs=[vmem, vmem],
        out_specs=(vmem, vmem, vmem),
    )(*results)
    return activated, weight_grad, bias_grad.reshape(256)


def solution(mesh):
    placed = (
        P("row", None),
        P("row", "rep", None, None, None, None),
        P("row", "rep", None, None, None),
        P("row", "rep", None),
        P(),
        P(),
        P(("row", "rep"), None),
    )
    return jax.shard_map(
        shards,
        mesh=mesh,
        in_specs=placed,
        out_specs=(P(("row", "rep"), None), P(), P()),
        check_vma=False,
    )
```

```python
import functools

import jax
import jax.numpy as jnp
from jax import lax
from jax.experimental import pallas as pl
from jax.experimental.pallas import tpu as pltpu
from jax.sharding import PartitionSpec as P

MESH = pl.DeviceIdType.MESH
F32 = jnp.float32
BF16 = jnp.bfloat16

PLANE = sorted(
    [(dx, dy) for dx in range(4) for dy in range(4) if (dx, dy) != (0, 0)],
    key=lambda o: -(min(o[0], 4 - o[0]) + min(o[1], 4 - o[1])),
)
ALONG_Z = [4, 3, 5, 2, 6, 1, 7]
GREETED = [(0, 0, 0, 1)] + [(d, 0, 0, 0) for d in (2, 1, 3)] + [(0, d, 0, 0) for d in (2, 1, 3)]


def layer_kernel(
    counts_hbm,
    coords_hbm,
    feat_hbm,
    adj_hbm,
    weight_hbm,
    bias_hbm,
    cot_hbm,
    act_ref,
    wg_ref,
    counts_ref,
    coords_ref,
    weight_ref,
    bias_ref,
    cot_ref,
    tiles,
    slot_rows,
    slots,
    held,
    feats,
    acc,
    part_out,
    part_in,
    c1_out,
    c1_in,
    b1_out,
    b1_in,
    c2_in,
    c3_in,
    load_sem,
    slot_sem,
    a1_send,
    a1_recv,
    a2_send,
    a2_recv,
    a3_send,
    a3_recv,
    b_send,
    b_recv,
    c_send,
    c_recv,
):
    row = lax.axis_index("row")
    rep = lax.axis_index("rep")
    xh, z, core = row // 16, (row // 2) % 8, row % 2
    xl, y = rep // 4, rep % 4
    x = xh * 2 + xl
    plane = x * 4 + y
    live = tiles.shape[0] - 1

    def device(dx, dy, dz, dcore):
        x2, y2, z2, c2 = (x + dx) % 4, (y + dy) % 4, (z + dz) % 8, (core + dcore) % 2
        return (x2 // 2) * 16 + z2 * 2 + c2, (x2 % 2) * 4 + y2

    def remote(src, dst, send, recv, target):
        return pltpu.make_async_remote_copy(
            src_ref=src,
            dst_ref=dst,
            send_sem=send,
            recv_sem=recv,
            device_id=target,
            device_id_type=MESH,
        )

    def wait_bytes(ref, sem):
        pltpu.make_async_copy(ref, ref, sem).wait()

    barrier = pltpu.get_barrier_semaphore()
    odd_z = (z + y // 2) % 2
    other_core = (core + y) % 2

    def greet(*offset):
        pl.semaphore_signal(barrier, inc=1, device_id=device(*offset), device_id_type=MESH)

    greet(0, 0, 2 - odd_z, 0)
    greet(0, 0, 6 + odd_z, 0)

    @pl.when(other_core == 1)
    def _():
        greet(0, 0, 2 - odd_z, 1)
        greet(0, 0, 6 + odd_z, 1)

    for offset in GREETED:
        greet(*offset)

    pending = []
    loads = [
        pltpu.make_async_copy(src, dst, load_sem.at[n])
        for n, (src, dst) in enumerate(
            [
                (counts_hbm, counts_ref),
                (coords_hbm, coords_ref),
                (adj_hbm, tiles.at[pl.ds(0, live)]),
                (weight_hbm, weight_ref),
                (bias_hbm, bias_ref),
                (cot_hbm, cot_ref),
            ]
        )
    ]
    tile_copy = loads[2]
    for load in loads:
        if load is not tile_copy:
            load.start()

    tiles[live] = jnp.zeros(tiles.shape[1:], BF16)
    lane = lax.broadcasted_iota(jnp.int32, (64, 32), 1)
    sub = lax.broadcasted_iota(jnp.int32, (64, 32), 0)
    wide_lane = lax.broadcasted_iota(jnp.int32, (64, 128), 1)
    wide_sub = lax.broadcasted_iota(jnp.int32, (64, 128), 0)
    loads[0].wait()
    loads[1].wait()
    for t in range(4):
        key = coords_ref[t, 0:1, :] * 8 + coords_ref[t, 1:2, :]
        hit = jnp.logical_and(key == sub, lane < counts_ref[0:1, t : t + 1])
        found = jnp.sum(jnp.where(hit, lane + (t * 32 + 1), 0), axis=1, keepdims=True)
        turned = jnp.sum(jnp.where(wide_lane == wide_sub, found, 0), axis=0, keepdims=True)
        slot_rows[t : t + 1, :] = jnp.where(turned == 0, live, turned - 1)
    slot_copy = pltpu.make_async_copy(slot_rows, slots, slot_sem)
    slot_copy.start()

    b1_out[...] = jnp.zeros_like(b1_out)
    acc[...] = jnp.zeros_like(acc)
    part_in[rep] = jnp.zeros(part_in.shape[1:], BF16)
    pl.semaphore_wait(barrier, len(GREETED) + (1 - odd_z) * (8 - 4 * other_core))

    even = z % 2 == y // 2
    source = jnp.logical_and(even, core == y % 2)

    def along_z(n, dz, to_core, first=0, count=2):
        return remote(
            feat_hbm.at[pl.ds(xl * 4 + to_core * 2 + first, count)],
            held.at[z, pl.ds(first, count)],
            a1_send.at[n],
            a1_recv.at[z, first],
            (xh * 16 + ((z + dz) % 8) * 2 + to_core, rep),
        )

    def own_quarter():
        return pltpu.make_async_copy(
            feat_hbm.at[pl.ds(xl * 4 + core * 2, 2)], held.at[z], a1_recv.at[z, 0]
        )

    def to_column(start):
        parts = [(2, 1, 1), (6, 0, 1), (1, 0, 1), (7, 0, 1), (2, 0, 1), (6, 1, 1), (1, 1, 1), (7, 1, 1)]
        copies = [
            along_z(2 * n + to_core, dz, to_core, first, count)
            for n, (dz, first, count) in enumerate(parts)
            for to_core in (0, 1)
        ]
        for copy in copies + [along_z(16, 0, 1 - core)]:
            copy.start() if start else copy.wait_send()

    pl.when(source)(lambda: (own_quarter().start(), to_column(True)) and None)
    tile_copy.start()
    pending.append(lambda: pl.when(source)(lambda: to_column(False)))

    def pass_along(dz, half, start):
        src = (z + dz) % 8
        piece = held.at[src, pl.ds(half, 1)]
        side = 1 if dz == 6 else -1
        for n, far in enumerate((1, 2)):
            if far == 1 or half == (dz == 6):
                send = a1_send.at[17 + (dz // 4) * 4 + half * 2 + n]
                copy = remote(piece, piece, send, a1_recv.at[src, half], device(0, 0, side * far, 0))
                copy.start() if start else copy.wait_send()

    def to_users(dz, first, count, start=True):
        src = (z + dz) % 8
        user_xl = (src % 4) // 2
        section = xh * 2 + src // 4
        piece = held.at[src, pl.ds(first, count)]
        place = feats.at[section, xl, core, pl.ds(first, count)]

        def send(n, target_xh):
            copy = remote(
                piece,
                place,
                a2_send.at[dz, n, first],
                a2_recv.at[section],
                (target_xh * 16 + z * 2 + core, user_xl * 4 + y),
            )
            copy.start() if start else copy.wait_send()

        send(0, 1 - xh)
        pl.when(user_xl != xl)(lambda: send(1, xh))
        if start:

            @pl.when(user_xl == xl)
            def _():
                pltpu.make_async_copy(piece, place, a2_recv.at[section]).start()

    def wait_piece(dz, first, count):
        src = (z + dz) % 8
        wait_bytes(held.at[src, pl.ds(first, count)], a1_recv.at[src, first])

    even_parts = [(0, 0, 2), (2, 0, 1), (6, 1, 1), (2, 1, 1), (6, 0, 1), (4, 0, 1), (4, 1, 1)]
    odd_parts = [(1, 0, 1), (7, 0, 1), (1, 1, 1), (7, 1, 1), (3, 0, 1), (5, 1, 1), (3, 1, 1), (5, 0, 1)]

    @pl.when(even)
    def _():
        for dz, first, count in even_parts:
            wait_piece(dz, first, count)
            if dz in (2, 6):
                pass_along(dz, first, True)
            to_users(dz, first, count)

    @pl.when(jnp.logical_not(even))
    def _():
        for dz, first, count in odd_parts:
            wait_piece(dz, first, count)
            to_users(dz, first, count)

    def drain_even():
        for part in even_parts:
            if part[0] in (2, 6):
                pass_along(part[0], part[1], False)
            to_users(*part, start=False)

    def drain_odd():
        for part in odd_parts:
            to_users(*part, start=False)

    pending.append(lambda: pl.when(even)(drain_even))
    pending.append(lambda: pl.when(jnp.logical_not(even))(drain_odd))

    nearer = ((rep // 2 - z + 10) % 8) // 5
    def pair(turn):
        th = (turn // 2 + nearer) % 2
        return xh * 2 + th, (1 - xh) * 2 + th

    def pass_on(section, start):
        piece = feats.at[section, pl.ds(0, 2), core]
        copy = remote(
            piece, piece, a3_send.at[section], a3_recv.at[section], device(0, 0, 0, 1)
        )
        if start:
            wait_bytes(piece, a2_recv.at[section])
            copy.start()
        else:
            copy.wait_send()

    def complete(section):
        wait_bytes(feats.at[section, pl.ds(0, 2), 1 - core], a3_recv.at[section])

    def products(r, sections, half):
        left, right = [], []
        for section in sections:
            for k in range(4):
                q = (k // 2) * 4 + half * 2 + k % 2
                left.append(tiles[slots[section, r * 8 + q]])
            right.append(feats[section, :, half].reshape(4 * 128, 128))
        return jnp.dot(
            jnp.concatenate(left, axis=1),
            jnp.concatenate(right, axis=0),
            preferred_element_type=F32,
        )

    tile_copy.wait()
    slot_copy.wait()
    tile_rows = [
        ((xl + 1 - i // 4) % 2) * 4 + (y + k) % 4 for i, k in enumerate((2, 1, 3, 0, 2, 1, 3, 0))
    ]

    def add_products(turn, carry):
        sections = pair(turn)

        @pl.when(turn % 2 == 0)
        def _():
            for section in sections:
                pass_on(section, True)

        @pl.when(turn % 2 == 1)
        def _():
            for section in sections:
                complete(section)

        for r in tile_rows:
            total = acc[r] + products(r, sections, (core + turn) % 2)
            acc[r] = total
            part_out[r] = total.astype(BF16)
        return carry

    pending.append(lambda: [pass_on(t, False) for t in range(4)])
    lax.fori_loop(0, 4, add_products, 0)
    for r in tile_rows[:7]:
        remote(part_out.at[r], part_in.at[rep], b_send, b_recv, (row, r)).start()
    total = acc[rep]

    for finish in pending:
        finish()
    pending.clear()
    pending.append(lambda: wait_bytes(part_out.at[pl.ds(0, 7)], b_send))
    wait_bytes(part_in.at[pl.ds(0, 7)], b_recv)
    for s in range(8):
        total = total + part_in[s].astype(F32)

    for load in loads[3:]:
        load.wait()
    aggregated = total.astype(BF16)
    pre = jnp.dot(aggregated, weight_ref[...], preferred_element_type=F32) + bias_ref[...]
    sig = jax.nn.sigmoid(pre)
    grad = (cot_ref[...].astype(F32) * sig * (1.0 + pre * (1.0 - sig))).astype(BF16)
    weight_part = lax.dot_general(
        aggregated, grad, (((0,), (0,)), ((), ())), preferred_element_type=F32
    )
    bias_part = jnp.sum(grad.astype(F32), axis=0, keepdims=True)

    first = plane == 0
    active = core == y % 2
    owner = jnp.logical_and(first, active)
    c1_out[0:8] = weight_part[:, 0:128].astype(BF16).reshape(8, 16, 128)
    c1_out[8:16] = weight_part[:, 128:256].astype(BF16).reshape(8, 16, 128)
    b1_out[0:1, :] = bias_part[:, 0:128]
    b1_out[1:2, :] = bias_part[:, 128:256]

    def send_bias():
        place = b1_in.at[plane * 2 + core]
        return remote(b1_out, place, c_send.at[3], c_recv.at[3], (z * 2, 0))

    def send_piece(dx, dy):
        x2, y2 = (x + dx) % 4, (y + dy) % 4
        target = (x2 // 2) * 16 + z * 2 + y2 % 2, (x2 % 2) * 4 + y2
        place = c1_in.at[plane * 2 + core]
        return remote(c1_out.at[x2 * 4 + y2], place, c_send.at[0], c_recv.at[0], target)

    for dx, dy in PLANE:
        send_piece(dx, dy).start()

    @pl.when(jnp.logical_not(owner))
    def _():
        send_bias().start()

    @pl.when(active)
    def _():
        c1_in[plane * 2 + core] = c1_out[plane]

    @pl.when(jnp.logical_not(active))
    def _():
        send_piece(0, 0).start()

    act_ref[...] = (pre * sig).astype(BF16)
    for finish in pending:
        finish()
    pending.clear()

    @pending.append
    def _():
        pl.when(jnp.logical_not(owner))(lambda: send_bias().wait_send())
        pl.when(active)(lambda: wait_bytes(c1_out.at[pl.ds(0, 15)], c_send.at[0]))
        pl.when(jnp.logical_not(active))(lambda: wait_bytes(c1_out, c_send.at[0]))

    pl.when(active)(lambda: wait_bytes(c1_in.at[pl.ds(0, 31)], c_recv.at[0]))

    def share_column(rows, start):
        piece = c2_in.at[z, pl.ds(0, rows)]
        for dz in ALONG_Z + [0]:
            for dcore in (0, 1):
                if dz or dcore:
                    copy = remote(
                        piece, piece, c_send.at[1], c_recv.at[1], device(0, 0, dz, dcore)
                    )
                    copy.start()

    def column_bytes(count, sem):
        pl.when(first)(lambda: wait_bytes(c2_in.at[pl.ds(0, count)], sem))
        pl.when(jnp.logical_not(first))(
            lambda: wait_bytes(c2_in.at[pl.ds(0, count), pl.ds(0, 16)], sem)
        )

    @pl.when(active)
    def _():
        c2_in[z, 0:16] = jnp.sum(c1_in[...].astype(F32), axis=0).astype(BF16)

        @pl.when(first)
        def _():
            b1_in[0] = b1_out[...]
            wait_bytes(b1_in.at[pl.ds(0, 31)], c_recv.at[3])
            both = jnp.sum(b1_in[...], axis=0)
            c2_in[z, 16:32] = jnp.concatenate([both, jnp.zeros_like(both)], axis=0).astype(BF16)
            share_column(32, True)

        pl.when(jnp.logical_not(first))(lambda: share_column(16, True))

    for finish in pending:
        finish()
    pending.clear()
    pl.when(active)(lambda: column_bytes(7, c_recv.at[1]))
    pl.when(jnp.logical_not(active))(lambda: column_bytes(8, c_recv.at[1]))

    @pl.when(first)
    def _():
        c3_in[0, 16:32] = jnp.sum(c2_in[:, 16:32].astype(F32), axis=0).astype(BF16)

    @pending.append
    def _():
        pl.when(active)(lambda: (column_bytes(8, c_send.at[1]), column_bytes(7, c_send.at[1])) and None)

    c3_in[plane, 0:16] = jnp.sum(c2_in[:, 0:16].astype(F32), axis=0).astype(BF16)

    @pl.when(first)
    def _():
        for dx, dy in PLANE:
            remote(
                c3_in.at[0], c3_in.at[0], c_send.at[2], c_recv.at[4], device(dx, dy, 0, 0)
            ).start()
        for finish in pending:
            finish()
        wait_bytes(c3_in.at[pl.ds(0, 15), pl.ds(0, 16)], c_recv.at[2])

    @pl.when(jnp.logical_not(first))
    def _():
        piece = c3_in.at[plane, pl.ds(0, 16)]
        for dx, dy in PLANE:
            remote(piece, piece, c_send.at[2], c_recv.at[2], device(dx, dy, 0, 0)).start()
        for finish in pending:
            finish()
        wait_bytes(c3_in.at[pl.ds(0, 14), pl.ds(0, 16)], c_recv.at[2])
        wait_bytes(c3_in.at[0], c_recv.at[4])

    pending.clear()

    @pending.append
    def _():
        pl.when(first)(lambda: wait_bytes(c3_in.at[pl.ds(0, 15)], c_send.at[2]))
        pl.when(jnp.logical_not(first))(
            lambda: wait_bytes(c3_in.at[pl.ds(0, 15), pl.ds(0, 16)], c_send.at[2])
        )

    wg_ref[...] = c3_in[...]

    for finish in pending:
        finish()


def hand_out(act_in, pieces, act_ref, wg_ref, bg_ref):
    act_ref[...] = act_in[...]
    wg_ref[:, 0:128] = pieces[0:8, 0:16].astype(F32).reshape(128, 128)
    wg_ref[:, 128:256] = pieces[8:16, 0:16].astype(F32).reshape(128, 128)
    bias_rows = pieces[0, 16:32].astype(F32)
    bg_ref[:, 0:128] = bias_rows[0:1]
    bg_ref[:, 128:256] = bias_rows[1:2]


def shards(features, adj_tiles, tile_coords, tile_counts, weight, out_bias, out_grad):
    vmem = pl.BlockSpec(memory_space=pltpu.VMEM)
    dma = pltpu.SemaphoreType.DMA
    outs = (
        jax.ShapeDtypeStruct((128, 256), BF16),
        jax.ShapeDtypeStruct((128, 256), F32),
        jax.ShapeDtypeStruct((1, 256), F32),
    )
    results = pl.pallas_call(
        layer_kernel,
        name="layer",
        out_shape=(outs[0], jax.ShapeDtypeStruct((16, 32, 128), BF16)),
        in_specs=[pl.BlockSpec(memory_space=pl.ANY)] * 7,
        out_specs=(vmem, vmem),
        scratch_shapes=[
            pltpu.VMEM((1, 4), jnp.int32),
            pltpu.VMEM((4, 2, 32), jnp.int32),
            pltpu.VMEM((128, 256), BF16),
            pltpu.VMEM((1, 256), F32),
            pltpu.VMEM((128, 256), BF16),
            pltpu.VMEM((129, 128, 128), BF16),
            pltpu.VMEM((4, 128), jnp.int32),
            pltpu.SMEM((4, 128), jnp.int32),
            pltpu.VMEM((8, 2, 128, 128), BF16),
            pltpu.VMEM((4, 2, 2, 2, 128, 128), BF16),
            pltpu.VMEM((8, 128, 128), F32),
            pltpu.VMEM((8, 128, 128), BF16),
            pltpu.VMEM((8, 128, 128), BF16),
            pltpu.VMEM((16, 16, 128), BF16),
            pltpu.VMEM((32, 16, 128), BF16),
            pltpu.VMEM((8, 128), F32),
            pltpu.VMEM((32, 8, 128), F32),
            pltpu.VMEM((8, 32, 128), BF16),
            pltpu.VMEM((16, 32, 128), BF16),
            dma((6,)),
            dma,
            dma((25,)),
            dma((8, 2)),
            dma((8, 2, 2)),
            dma((4,)),
            dma((4,)),
            dma((4,)),
            dma,
            dma,
            dma((5,)),
            dma((6,)),
        ],
        compiler_params=pltpu.CompilerParams(
            collective_id=1, has_side_effects=True, vmem_limit_bytes=60 << 20
        ),
        cost_estimate=pl.CostEstimate(
            flops=2 * 256 * 128**3, bytes_accessed=5 << 20, transcendentals=128 * 256
        ),
    )(
        tile_counts.reshape(1, 4),
        jnp.swapaxes(tile_coords[0, 0], 1, 2),
        features.reshape(8, 128, 128),
        adj_tiles.reshape(128, 128, 128),
        weight,
        out_bias.reshape(1, 256),
        out_grad,
    )
    activated, weight_grad, bias_grad = pl.pallas_call(
        hand_out,
        name="hand_out",
        out_shape=outs,
        in_specs=[vmem, vmem],
        out_specs=(vmem, vmem, vmem),
    )(*results)
    return activated, weight_grad, bias_grad.reshape(256)


def solution(mesh):
    placed = (
        P("row", None),
        P("row", "rep", None, None, None, None),
        P("row", "rep", None, None, None),
        P("row", "rep", None),
        P(),
        P(),
        P(("row", "rep"), None),
    )
    return jax.shard_map(
        shards,
        mesh=mesh,
        in_specs=placed,
        out_specs=(P(("row", "rep"), None), P(), P()),
        check_vma=False,
    )
```
